512 devices in a mesh: inner: 16 (over z_lo, y), blk: 32 (over x, z_hi, core).
Axes of the slice: x: 4, y: 8, z: 8 (z_hi: 4, z_lo: 2; z = z_hi * 2 + z_lo), core: 2. Of those that a mesh axis runs over, the one named last changes fastest.
Arguments:
- image_emb: float32 [12288, 768], P(('inner', 'blk')), may hold values from -150 to 150
- text_emb: float32 [12288, 768], P(('inner', 'blk')), may hold values from -150 to 150
- logit_scale: float32 [1], replicated, may hold values from 30 to 100
Outputs:
- mean_loss: float32 [1], replicated
- image_grad: float32 [12288, 768], P(('inner', 'blk'))
- text_grad: float32 [12288, 768], P(('inner', 'blk'))
The draws below stay inside these ranges and needn't reach their ends.
All inputs are finite; a program needn't handle non-finite values.
Results may differ from the reference program's by a relative error of at most 0.006.
Values may be sent and summed in bfloat16 or wider, within the bound.
No kernel may reach another device: no remote copies, remote signals or barrier semaphores. Data moves between devices by JAX's collectives and lax.ppermute only.
A program may use at most 64 MiB of HBM per device.

```python
import jax
import jax.numpy as jnp
from jax import lax

E = 768
BATCH = 12288


def embed_pair(key):
    keys = jax.random.split(jax.random.fold_in(key, 4242), 5)
    image_noise = jax.random.truncated_normal(keys[0], -5.0, 5.0, (BATCH, E), jnp.float32)
    text_noise = jax.random.truncated_normal(keys[1], -5.0, 5.0, (BATCH, E), jnp.float32)
    image_spread = jnp.exp(jax.random.uniform(keys[3], (BATCH, 1), jnp.float32) * jnp.log(10.0))
    text_spread = jnp.exp(jax.random.uniform(keys[4], (BATCH, 1), jnp.float32) * jnp.log(10.0))
    image_rows = image_noise
    text_rows = text_noise
    return (image_rows * image_spread, text_rows * text_spread)


def draw_image_emb(key, part):
    return embed_pair(key)[0]


def draw_text_emb(key, part):
    return embed_pair(key)[1]


def draw_logit_scale(key, part):
    sample = jax.random.uniform(jax.random.fold_in(key, 99), (1,), jnp.float32)
    return jnp.exp(jnp.log(30.0) + sample * jnp.log(100.0 / 30.0))


def setup_inputs(seed: int = 0) -> dict:
    splits = jax.random.split(jax.random.key(seed), 4)
    return {
        "image_emb": draw_image_emb(jax.random.fold_in(splits[3], 71), 0),
        "text_emb": draw_text_emb(jax.random.fold_in(splits[3], 71), 0),
        "logit_scale": draw_logit_scale(jax.random.fold_in(splits[3], 71), 0),
    }


EPSILON = 1e-06

def unit_rows(values):
    inverse = lax.rsqrt(lax.optimization_barrier(jnp.sum(values * values, axis=1, keepdims=True)) + EPSILON)
    return (values * inverse, inverse)

def project(gradient, direction, inverse):
    return (gradient - direction * lax.optimization_barrier(jnp.sum(gradient * direction, axis=1, keepdims=True))) * inverse

def reference(image_emb, text_emb, logit_scale):
    factor = logit_scale[0]
    image_unit, image_inverse = unit_rows(image_emb)
    text_unit, text_inverse = unit_rows(text_emb)
    image_half = image_unit.astype(jnp.bfloat16)
    text_half = text_unit.astype(jnp.bfloat16)
    count_rows = image_emb.shape[0]
    embed_width = image_emb.shape[1]
    text_blocks = text_half.reshape(16, count_rows // 16, embed_width)

    def scores(text_block):
        return factor * jnp.dot(image_half, text_block.T, preferred_element_type=jnp.float32)

    def stats_step(state, text_block):
        row_peak, row_total = state
        logits = scores(text_block)
        new_peak = jnp.maximum(row_peak, lax.optimization_barrier(jnp.max(logits, axis=1)))
        row_total = row_total * jnp.exp(row_peak - new_peak) + lax.optimization_barrier(jnp.sum(jnp.exp(logits - new_peak[:, None]), axis=1))
        col_peak = lax.optimization_barrier(jnp.max(logits, axis=0))
        col_lse = col_peak + jnp.log(lax.optimization_barrier(jnp.sum(jnp.exp(logits - col_peak[None, :]), axis=0)))
        return ((new_peak, row_total), col_lse)
    initial = (jnp.full((count_rows,), -1e+30, jnp.float32), jnp.zeros((count_rows,), jnp.float32))
    (row_peak, row_total), col_parts = lax.scan(stats_step, initial, text_blocks)
    row_lse = row_peak + jnp.log(row_total)
    col_lse = col_parts.reshape(count_rows)

    def grad_step(image_acc, inputs):
        text_block, col_block = inputs
        logits = scores(text_block)
        weights = (0.5 * factor * (jnp.exp(logits - row_lse[:, None]) + jnp.exp(logits - col_block[None, :]))).astype(jnp.bfloat16)
        image_acc = image_acc + jnp.dot(weights, text_block, preferred_element_type=jnp.float32)
        text_part = jnp.dot(weights.T, image_half, preferred_element_type=jnp.float32)
        return (image_acc, text_part)
    image_sum, text_parts = lax.scan(grad_step, jnp.zeros((count_rows, embed_width), jnp.float32), (text_blocks, col_lse.reshape(16, count_rows // 16)))
    text_sum = text_parts.reshape(count_rows, embed_width)
    diagonal = factor * lax.optimization_barrier(jnp.sum(image_half.astype(jnp.float32) * text_half.astype(jnp.float32), axis=1))
    mean_loss = (jnp.sum(row_lse - diagonal) + jnp.sum(col_lse - diagonal)) / (2.0 * count_rows)
    image_pull = image_sum - factor * text_half.astype(jnp.float32)
    text_pull = text_sum - factor * image_half.astype(jnp.float32)
    return (mean_loss.reshape(1), project(image_pull, image_unit, image_inverse), project(text_pull, text_unit, text_inverse))
```

```python
import functools

import jax
import jax.numpy as jnp
from jax import lax
from jax.experimental import pallas as pl
from jax.experimental.pallas import tpu as pltpu
from jax.sharding import Mesh
from jax.sharding import PartitionSpec as P

INNER = ("z0", "y2", "y1", "y0")
CHIPS = ("x", "zh")
CORE = "c"
BLK = ("x", "zh", "c")
ALL = ("z0", "y2", "y1", "y0", "x", "zh", "c")

EPSILON = 1e-06
LAST = (((1,), (1,)), ((), ()))
FIRST = (((0,), (0,)), ((), ()))
VMEM_LIMIT = 48 * 1024 * 1024


def f32_dot(a, b, dims):
    return lax.dot_general(a, b, dims, preferred_element_type=jnp.float32)


def unit_rows(values):
    inverse = lax.rsqrt(jnp.sum(values * values, axis=1, keepdims=True) + EPSILON)
    return values * inverse, inverse


def kernel_call(body, out_shape, *args, flops=0):
    in_specs = [
        pl.BlockSpec(memory_space=pltpu.SMEM if a.size == 1 else pltpu.VMEM) for a in args
    ]
    outs = jax.tree.leaves(out_shape)
    moved = sum(a.size * a.dtype.itemsize for a in (*args, *outs))
    return pl.pallas_call(
        body,
        out_shape=out_shape,
        in_specs=in_specs,
        compiler_params=pltpu.CompilerParams(vmem_limit_bytes=VMEM_LIMIT),
        cost_estimate=pl.CostEstimate(flops=flops, bytes_accessed=moved, transcendentals=0),
    )(*args)


def units_kernel(values_ref, copies_ref):
    unit, _ = unit_rows(values_ref[...])
    half = jnp.concatenate([unit, unit], axis=0).astype(jnp.bfloat16)
    rows = half.shape[0]
    for k in range(copies_ref.shape[0] // rows):
        copies_ref[k * rows : (k + 1) * rows, :] = half


def units_and_diagonal_kernel(values_ref, other_ref, copies_ref, diagonal_ref):
    units_kernel(values_ref, copies_ref)
    first = unit_rows(values_ref[...])[0].astype(jnp.bfloat16).astype(jnp.float32)
    second = unit_rows(other_ref[...])[0].astype(jnp.bfloat16).astype(jnp.float32)
    diagonal_ref[...] = jnp.broadcast_to(jnp.sum(first * second), diagonal_ref.shape)


def lines(row):
    return [row[:, k * 128 : (k + 1) * 128] for k in range(row.shape[1] // 128)]


def lse_of(parts):
    peak = functools.reduce(jnp.maximum, [jnp.max(p, axis=0, keepdims=True) for p in parts])
    total = sum(jnp.sum(jnp.exp(p - peak), axis=0, keepdims=True) for p in parts)
    return peak + jnp.log(total)


def stats_kernel(factor_ref, core_ref, image_ref, own_ref, other_ref, diagonal_ref, row_ref, col_ref):
    factor = factor_ref[0]
    image, own, other = image_ref[...], own_ref[...], other_ref[...]
    own_lse = lse_of([factor * f32_dot(image, own, LAST)])
    other_lse = lse_of([factor * f32_dot(image, other, LAST)])
    row_lse = lse_of([factor * f32_dot(own, image, LAST), factor * f32_dot(other, image, LAST)])
    zero = jnp.zeros((1, 128), jnp.float32)
    rows = lines(row_lse)
    diagonal = factor * diagonal_ref[0:1, :]
    message = jnp.concatenate([*rows, diagonal, *[zero] * (7 - len(rows))], axis=0)
    row_ref[...] = jnp.broadcast_to(message[None], row_ref.shape)
    first_core = core_ref[0] == 0
    cols = lines(jnp.where(first_core, own_lse, other_lse)) + lines(
        jnp.where(first_core, other_lse, own_lse)
    )
    col_ref[...] = jnp.concatenate([*cols, *[zero] * (8 - len(cols))], axis=0)


def pieces_lse(pieces):
    peak = jnp.max(pieces, axis=0)
    return peak + jnp.log(jnp.sum(jnp.exp(pieces - peak[None]), axis=0))


def middle_kernel(pieces_ref, col_ref, row_ref, message_ref):
    pieces = pieces_ref[...]
    lse = pieces_lse(pieces)
    diagonal = jnp.sum(pieces[:, 3:4, 0:1])
    share = jnp.sum(lse[0:3, :]) - 2.0 * diagonal
    row_ref[...] = lse
    place = lax.broadcasted_iota(jnp.int32, (8, 128), 0)
    message = jnp.where(place == 6, share, col_ref[...])
    message_ref[...] = jnp.broadcast_to(message[None], message_ref.shape)


def weights_kernel(
    factor_ref, core_ref, image_ref, own_ref, other_ref, row_ref, pieces_ref,
    image_out, own_out, other_out, share_ref,
):
    factor = factor_ref[0]
    pieces = pieces_ref[...]
    cols = pieces_lse(pieces)
    share_ref[0:8, :] = jnp.broadcast_to(jnp.sum(cols[0:6, :]), (8, 128))
    share_ref[8:16, :] = jnp.broadcast_to(jnp.sum(pieces[:, 6:7, 0:1]), (8, 128))
    core0 = jnp.concatenate([cols[k : k + 1, :] for k in range(3)], axis=1)
    core1 = jnp.concatenate([cols[k : k + 1, :] for k in range(3, 6)], axis=1)
    first_core = core_ref[0] == 0
    row_lse = jnp.concatenate(
        [jnp.transpose(jnp.broadcast_to(row_ref[k : k + 1, :], (128, 128))) for k in range(3)],
        axis=0,
    )[:, 0:1]
    image = image_ref[...]
    image_sum = None
    for mine, text_ref in ((True, own_ref), (False, other_ref)):
        text = text_ref[...]
        col_lse = jnp.where(first_core == mine, core0, core1)
        logits = factor * f32_dot(image, text, LAST)
        weights = (
            (0.5 * factor) * (jnp.exp(logits - row_lse) + jnp.exp(logits - col_lse))
        ).astype(jnp.bfloat16)
        part = jnp.dot(weights, text, preferred_element_type=jnp.float32)
        image_sum = part if image_sum is None else image_sum + part
        text_sum = f32_dot(weights, image, FIRST)
        if mine:
            own_out[...] = text_sum
        else:
            other_out[...] = text_sum.astype(jnp.bfloat16)
    image_out[...] = image_sum.astype(jnp.bfloat16)


def gradient_kernel(factor_ref, values_ref, paired_ref, pieces_ref, gradient_ref):
    unit, inverse = unit_rows(values_ref[...])
    paired = unit_rows(paired_ref[...])[0].astype(jnp.bfloat16).astype(jnp.float32)
    rows = unit.shape[0]
    total = None
    for k in range(pieces_ref.shape[0] // (2 * rows)):
        both = pieces_ref[2 * rows * k : 2 * rows * (k + 1), :].astype(jnp.float32)
        both = both[:rows] + both[rows:]
        total = both if total is None else total + both
    pull = total - factor_ref[0] * paired
    gradient_ref[...] = (pull - unit * jnp.sum(pull * unit, axis=1, keepdims=True)) * inverse


def exchanged(blocks, axis):
    count = lax.axis_size(axis)
    split = blocks.reshape(count, -1, *blocks.shape[1:])
    return lax.all_to_all(split, axis, split_axis=0, concat_axis=0, tiled=True).reshape(blocks.shape)


def swapped(x, axis):
    return lax.ppermute(x, axis, [(0, 1), (1, 0)])


def shape(dims, dtype):
    return jax.ShapeDtypeStruct(dims, dtype)


def on_device(image_emb, text_emb, factor):
    own_rows, width = image_emb.shape
    inner, chips, blk = (lax.axis_size(a) for a in (INNER, CHIPS, BLK))
    core = lax.axis_index(CORE).astype(jnp.int32).reshape(1)
    bf16, f32 = jnp.bfloat16, jnp.float32
    image_rows, text_rows = own_rows * inner, own_rows * chips
    work = 2 * image_rows * text_rows * width

    text_copies = kernel_call(units_kernel, shape((text_rows, width), bf16), text_emb)
    text_own = exchanged(text_copies, CHIPS)
    text_other = swapped(text_own, CORE)
    image_copies, diagonal = kernel_call(
        units_and_diagonal_kernel,
        (shape((image_rows, width), bf16), shape((8, 128), f32)),
        image_emb,
        text_emb,
    )
    image_copies, _ = lax.optimization_barrier((image_copies, text_own))
    image_group = exchanged(image_copies, INNER)

    row_message, col_part = kernel_call(
        stats_kernel,
        (shape((inner, 8, 128), f32), shape((8, 128), f32)),
        factor, core, image_group, text_own, text_other, diagonal,
        flops=4 * work,
    )
    row_pieces = exchanged(row_message, INNER)
    row_lse, col_message = kernel_call(
        middle_kernel, (shape((8, 128), f32), shape((blk, 8, 128), f32)), row_pieces, col_part
    )
    col_pieces = exchanged(col_message, BLK)

    image_part, own_part, other_part, shares = kernel_call(
        weights_kernel,
        (
            shape((image_rows, width), bf16),
            shape((text_rows, width), f32),
            shape((text_rows, width), bf16),
            shape((16, 128), f32),
        ),
        factor, core, image_group, text_own, text_other, row_lse, col_pieces,
        flops=6 * work,
    )
    swapped_part = swapped(other_part, CORE)
    image_pieces = exchanged(image_part, INNER)
    text_part = (own_part + swapped_part.astype(f32)).astype(bf16)
    text_part, _ = lax.optimization_barrier((text_part, image_pieces))
    text_pieces = exchanged(text_part, CHIPS)

    col_share = shares[0:8]
    for axis in INNER:
        col_share = col_share + swapped(col_share, axis)
    whole = 2.0 * own_rows * inner * blk
    mean_loss = ((col_share[0, 0] + shares[8, 0]) / whole).reshape(1)

    out = shape((own_rows, width), f32)
    image_grad = kernel_call(gradient_kernel, out, factor, image_emb, text_emb, image_pieces)
    text_grad = kernel_call(gradient_kernel, out, factor, text_emb, image_emb, text_pieces)
    return (mean_loss, image_grad, text_grad)


def solution(mesh):
    split = Mesh(mesh.devices.reshape(2, 2, 2, 2, 4, 4, 2), ALL)
    in_specs = (P(ALL, None), P(ALL, None), P())
    out_specs = (P(), P(ALL, None), P(ALL, None))
    return jax.shard_map(
        on_device, mesh=split, in_specs=in_specs, out_specs=out_specs, check_vma=False
    )
```

```python
import functools

import jax
import jax.numpy as jnp
from jax import lax
from jax.experimental import pallas as pl
from jax.experimental.pallas import tpu as pltpu
from jax.sharding import Mesh
from jax.sharding import PartitionSpec as P

ALL = ("z0", "y2", "y1", "y0", "x", "zh", "c")
INNER = ("z0", "y2", "y1", "y0")
CHIPS = ("x", "zh")
NEAR = ("z0", "y0")
NEAR_STATS = ("z0", "y0", "y1")
MIDDLE = "y1"
FAR = "y2"
CORE = "c"

EPSILON = 1e-06
LAST = (((1,), (1,)), ((), ()))
FIRST = (((0,), (0,)), ((), ()))
VMEM_LIMIT = 24 * 1024 * 1024
EXTRA = 128


def f32_dot(a, b, dims):
    return lax.dot_general(a, b, dims, preferred_element_type=jnp.float32)


def unit_rows(values):
    inverse = lax.rsqrt(jnp.sum(values * values, axis=1, keepdims=True) + EPSILON)
    return values * inverse, inverse


def kernel_call(body, out_shape, *args, flops=0):
    def spec(a):
        return pl.BlockSpec(memory_space=pltpu.SMEM if a.size == 1 else pltpu.VMEM)

    outs = jax.tree.leaves(out_shape)
    moved = sum(a.size * a.dtype.itemsize for a in (*args, *outs))
    return pl.pallas_call(
        body,
        out_shape=out_shape,
        in_specs=[spec(a) for a in args],
        out_specs=jax.tree.map(spec, out_shape),
        compiler_params=pltpu.CompilerParams(vmem_limit_bytes=VMEM_LIMIT),
        cost_estimate=pl.CostEstimate(flops=flops, bytes_accessed=moved, transcendentals=0),
    )(*args)


def packed(value, rows):
    value = jnp.broadcast_to(value, (rows, EXTRA))
    high = value.astype(jnp.bfloat16).astype(jnp.float32)
    middle = (value - high).astype(jnp.bfloat16).astype(jnp.float32)
    low = value - high - middle
    lane = lax.broadcasted_iota(jnp.int32, (rows, EXTRA), 1)
    parts = jnp.where(lane == 0, high, jnp.where(lane == 1, middle, jnp.where(lane == 2, low, 0.0)))
    return parts.astype(jnp.bfloat16)


def unpacked(values, width):
    return jnp.sum(values[0:1, width:])


def text_units_kernel(values_ref, copies_ref):
    unit, _ = unit_rows(values_ref[...])
    half = jnp.concatenate([unit, unit], axis=0).astype(jnp.bfloat16)
    rows = half.shape[0]
    for k in range(copies_ref.shape[0] // rows):
        copies_ref[k * rows : (k + 1) * rows, :] = half


def image_units_kernel(values_ref, other_ref, half_ref, diagonal_ref):
    first = unit_rows(values_ref[...])[0].astype(jnp.bfloat16)
    second = unit_rows(other_ref[...])[0].astype(jnp.bfloat16)
    half_ref[...] = first
    products = first.astype(jnp.float32) * second.astype(jnp.float32)
    diagonal_ref[...] = jnp.broadcast_to(jnp.sum(products), diagonal_ref.shape)


def join_kernel(side_ref, mine_ref, theirs_ref, joined_ref):
    mine, theirs = mine_ref[...].astype(jnp.float32), theirs_ref[...].astype(jnp.float32)
    first = side_ref[0] == 0
    joined = jnp.concatenate(
        [jnp.where(first, mine, theirs), jnp.where(first, theirs, mine)], axis=0
    ).astype(jnp.bfloat16)
    rows = joined.shape[0]
    for k in range(joined_ref.shape[0] // rows):
        joined_ref[k * rows : (k + 1) * rows, :] = joined


def lines(row):
    return [row[:, k * 128 : (k + 1) * 128] for k in range(row.shape[1] // 128)]


def line(rows):
    return jnp.concatenate([rows[k : k + 1, :] for k in range(rows.shape[0])], axis=1)


def eight(rows):
    zero = jnp.zeros((1, 128), jnp.float32)
    return jnp.concatenate([*rows, *[zero] * (8 - len(rows))], axis=0)


def lse_of(parts):
    peak = functools.reduce(jnp.maximum, [jnp.max(p, axis=0, keepdims=True) for p in parts])
    total = sum(jnp.sum(jnp.exp(p - peak), axis=0, keepdims=True) for p in parts)
    return peak + jnp.log(total)


def pieces_lse(pieces):
    peak = jnp.max(pieces, axis=0)
    return peak + jnp.log(jnp.sum(jnp.exp(pieces - peak[None]), axis=0))


def pair_lse(a, b):
    peak = jnp.maximum(a, b)
    return peak + jnp.log(jnp.exp(a - peak) + jnp.exp(b - peak))


def stats_kernel(factor_ref, image_ref, own_ref, other_ref, diagonal_ref, row_ref, col_ref):
    factor = factor_ref[0]
    image, own, other = image_ref[...], own_ref[...], other_ref[...]
    own_lse = lse_of([factor * f32_dot(image, own, LAST)])
    other_lse = lse_of([factor * f32_dot(image, other, LAST)])
    row_lse = lse_of([factor * f32_dot(own, image, LAST), factor * f32_dot(other, image, LAST)])
    message = eight([*lines(row_lse), factor * diagonal_ref[0:1, :]])
    row_ref[...] = jnp.broadcast_to(message[None], row_ref.shape)
    col_ref[...] = eight([*lines(own_lse), *lines(other_lse)])


def pair_columns_kernel(mine_ref, theirs_ref, message_ref):
    mine, theirs = mine_ref[...], theirs_ref[...]
    own = pair_lse(mine[0:3], theirs[3:6])
    other = pair_lse(mine[3:6], theirs[0:3])
    message = jnp.concatenate([own, other, jnp.zeros((2, 128), jnp.float32)], axis=0)
    message_ref[...] = jnp.broadcast_to(message[None], message_ref.shape)


def near_rows_kernel(pieces_ref, message_ref):
    pieces = pieces_ref[...]
    place = lax.broadcasted_iota(jnp.int32, (8, 128), 0)
    message_ref[...] = jnp.where(place == 3, jnp.sum(pieces, axis=0), pieces_lse(pieces))


def weights_kernel(
    factor_ref, image_ref, own_ref, other_ref, row_ref, far_row_ref, pieces_ref,
    image_out, own_out, other_out, share_ref,
):
    factor = factor_ref[0]
    width = own_ref.shape[1]
    cols = pieces_lse(pieces_ref[...])
    own_lse, other_lse = line(cols[0:3]), line(cols[3:6])
    col_share = jnp.sum(own_lse) + jnp.sum(other_lse)
    near, far = row_ref[...], far_row_ref[...]
    rows = pair_lse(near[0:3], far[0:3])
    row_share = jnp.sum(rows) - 2.0 * jnp.max(near[3:4] + far[3:4])
    share_ref[...] = jnp.broadcast_to(row_share, share_ref.shape)
    row_lse = jnp.concatenate(
        [jnp.transpose(jnp.broadcast_to(rows[k : k + 1, :], (128, 128))) for k in range(3)], axis=0
    )[:, 0:1]
    image = image_ref[...]
    image_sum = None
    for text_ref, col_lse in ((own_ref, own_lse), (other_ref, other_lse)):
        text = text_ref[...]
        logits = factor * f32_dot(image, text, LAST)
        weights = (
            (0.5 * factor) * (jnp.exp(logits - row_lse) + jnp.exp(logits - col_lse))
        ).astype(jnp.bfloat16)
        part = jnp.dot(weights, text, preferred_element_type=jnp.float32)
        image_sum = part if image_sum is None else image_sum + part
        text_sum = f32_dot(weights, image, FIRST)
        if text_ref is own_ref:
            own_out[...] = text_sum
        else:
            other_out[:, :width] = text_sum.astype(jnp.bfloat16)
    other_out[:, width:] = packed(row_share, other_out.shape[0])
    image_out[:, :width] = image_sum.astype(jnp.bfloat16)
    image_out[:, width:] = packed(col_share, image_out.shape[0])


def pair_sums_kernel(own_ref, theirs_ref, share_ref, message_ref):
    width = own_ref.shape[1]
    theirs = theirs_ref[...].astype(jnp.float32)
    message_ref[:, :width] = (own_ref[...] + theirs[:, :width]).astype(jnp.bfloat16)
    share = jnp.max(share_ref[...]) + unpacked(theirs, width)
    message_ref[:, width:] = packed(share, message_ref.shape[0])


def slabs_sum(pieces_ref, rows):
    total = None
    for k in range(pieces_ref.shape[0] // (2 * rows)):
        both = pieces_ref[2 * rows * k : 2 * rows * (k + 1), :].astype(jnp.float32)
        both = both[:rows] + both[rows:]
        total = both if total is None else total + both
    return total


def keep_and_send(total, share, side_ref, keep_ref, send_ref, share_ref):
    rows, width = keep_ref.shape
    first = side_ref[0] == 0
    lower, upper = total[:rows, :width], total[rows:, :width]
    keep_ref[...] = jnp.where(first, lower, upper)
    send_ref[:, :width] = jnp.where(first, upper, lower).astype(jnp.bfloat16)
    send_ref[:, width:] = packed(share, rows)
    share_ref[...] = jnp.broadcast_to(share, share_ref.shape)


def near_sums_kernel(side_ref, pieces_ref, keep_ref, send_ref, share_ref):
    rows, width = keep_ref.shape
    total = slabs_sum(pieces_ref, 2 * rows)
    keep_and_send(total, unpacked(total, width), side_ref, keep_ref, send_ref, share_ref)


def middle_sums_kernel(side_ref, kept_ref, theirs_ref, shared_ref, keep_ref, send_ref, share_ref):
    width = kept_ref.shape[1]
    theirs = theirs_ref[...].astype(jnp.float32)
    share = jnp.max(shared_ref[...]) + unpacked(theirs, width)
    keep_and_send(kept_ref[...] + theirs[:, :width], share, side_ref, keep_ref, send_ref, share_ref)


def gradient(factor, values, paired, total):
    unit, inverse = unit_rows(values)
    pull = total - factor * unit_rows(paired)[0].astype(jnp.bfloat16).astype(jnp.float32)
    return (pull - unit * jnp.sum(pull * unit, axis=1, keepdims=True)) * inverse


def image_gradient_kernel(
    factor_ref, values_ref, paired_ref, kept_ref, theirs_ref, shared_ref, gradient_ref, share_ref
):
    width = kept_ref.shape[1]
    theirs = theirs_ref[...].astype(jnp.float32)
    total = kept_ref[...] + theirs[:, :width]
    gradient_ref[...] = gradient(factor_ref[0], values_ref[...], paired_ref[...], total)
    share = jnp.max(shared_ref[...]) + unpacked(theirs, width)
    share_ref[...] = jnp.broadcast_to(share, share_ref.shape)


def text_gradient_kernel(
    factor_ref, values_ref, paired_ref, pieces_ref, shared_ref, gradient_ref, share_ref
):
    rows, width = values_ref.shape
    total = slabs_sum(pieces_ref, rows)
    gradient_ref[...] = gradient(
        factor_ref[0], values_ref[...], paired_ref[...], total[:, :width]
    )
    share = jnp.max(shared_ref[...]) + unpacked(total, width)
    share_ref[...] = jnp.broadcast_to(share, share_ref.shape)


def exchanged(blocks, axis):
    count = lax.axis_size(axis)
    split = blocks.reshape(count, -1, blocks.shape[-1])
    return lax.all_to_all(split, axis, split_axis=0, concat_axis=0, tiled=True).reshape(blocks.shape)


def swapped(x, axis):
    return lax.ppermute(x, axis, [(0, 1), (1, 0)])


def after(x, first):
    return lax.optimization_barrier((x, first))[0]


def shape(dims, dtype):
    return jax.ShapeDtypeStruct(dims, dtype)


def place(axis):
    return lax.axis_index(axis).astype(jnp.int32).reshape(1)


def on_device(image_emb, text_emb, factor):
    own_rows, width = image_emb.shape
    inner, chips, near = (lax.axis_size(a) for a in (INNER, CHIPS, NEAR))
    bf16, f32 = jnp.bfloat16, jnp.float32
    image_rows, text_rows = own_rows * inner, own_rows * chips
    wide = width + EXTRA
    work = 2 * image_rows * text_rows * width
    middle, far = place(MIDDLE), place(FAR)
    tile = shape((8, 128), f32)

    text_copies = kernel_call(text_units_kernel, shape((text_rows, width), bf16), text_emb)
    text_own = exchanged(text_copies, CHIPS)
    text_other = swapped(text_own, CORE)
    half, diagonal = kernel_call(
        image_units_kernel, (shape((own_rows, width), bf16), tile), image_emb, text_emb
    )
    two = kernel_call(
        join_kernel, shape((2 * own_rows, width), bf16), far, half, swapped(half, FAR)
    )
    image_copies = kernel_call(
        join_kernel, shape((image_rows, width), bf16), middle, two, swapped(two, MIDDLE)
    )
    image_group = exchanged(after(image_copies, text_own), NEAR)

    row_message, col_part = kernel_call(
        stats_kernel,
        (shape((lax.axis_size(NEAR_STATS), 8, 128), f32), tile),
        factor, image_group, text_own, text_other, diagonal,
        flops=4 * work,
    )
    row_pieces = exchanged(row_message, NEAR_STATS)
    col_message = kernel_call(
        pair_columns_kernel, shape((chips, 8, 128), f32), col_part, swapped(col_part, CORE)
    )
    col_pieces = exchanged(after(col_message, row_pieces), CHIPS)
    near_rows = kernel_call(near_rows_kernel, tile, row_pieces)

    image_part, own_part, other_part, row_share = kernel_call(
        weights_kernel,
        (
            shape((image_rows, wide), bf16),
            shape((text_rows, width), f32),
            shape((text_rows, wide), bf16),
            tile,
        ),
        factor, image_group, text_own, text_other, near_rows, swapped(near_rows, FAR), col_pieces,
        flops=6 * work,
    )
    image_pieces = exchanged(image_part, NEAR)
    text_part = kernel_call(
        pair_sums_kernel, shape((text_rows, wide), bf16),
        own_part, swapped(other_part, CORE), row_share,
    )
    text_pieces = exchanged(after(text_part, image_pieces), CHIPS)

    kept, sent, share = kernel_call(
        near_sums_kernel,
        (shape((2 * own_rows, width), f32), shape((2 * own_rows, wide), bf16), tile),
        middle, image_pieces,
    )
    kept, sent, share = kernel_call(
        middle_sums_kernel,
        (shape((own_rows, width), f32), shape((own_rows, wide), bf16), tile),
        far, kept, swapped(sent, MIDDLE), share,
    )
    out = shape((own_rows, width), f32)
    image_grad, share = kernel_call(
        image_gradient_kernel, (out, tile),
        factor, image_emb, text_emb, kept, swapped(sent, FAR), share,
    )
    text_grad, share = kernel_call(
        text_gradient_kernel, (out, tile), factor, text_emb, image_emb, text_pieces, share
    )
    whole = 2.0 * own_rows * inner * chips * lax.axis_size(CORE)
    return ((share[0, 0] / whole).reshape(1), image_grad, text_grad)


def solution(mesh):
    split = Mesh(mesh.devices.reshape(2, 2, 2, 2, 4, 4, 2), ALL)
    in_specs = (P(ALL, None), P(ALL, None), P())
    out_specs = (P(), P(ALL, None), P(ALL, None))
    return jax.shard_map(
        on_device, mesh=split, in_specs=in_specs, out_specs=out_specs, check_vma=False
    )
```

```python
import functools

import jax
import jax.numpy as jnp
from jax import lax
from jax.experimental import pallas as pl
from jax.experimental.pallas import tpu as pltpu
from jax.sharding import Mesh
from jax.sharding import PartitionSpec as P

ALL = ("z0", "y2", "y1", "y0", "x", "zh", "c")
INNER = ("z0", "y2", "y1", "y0")
CHIPS = ("x", "zh")
NEAR = ("z0", "y0", "y1")
FAR = "y2"
CORE = "c"

EPSILON = 1e-06
LAST = (((1,), (1,)), ((), ()))
FIRST = (((0,), (0,)), ((), ()))
VMEM_LIMIT = 24 * 1024 * 1024
EXTRA = 128
LOG2_E = 1.4426950408889634


def f32_dot(a, b, dims):
    return lax.dot_general(a, b, dims, preferred_element_type=jnp.float32)


def unit_rows(values):
    inverse = lax.rsqrt(jnp.sum(values * values, axis=1, keepdims=True) + EPSILON)
    return values * inverse, inverse


def kernel_call(body, out_shape, *args, flops=0):
    def spec(a):
        return pl.BlockSpec(memory_space=pltpu.SMEM if a.size == 1 else pltpu.VMEM)

    outs = jax.tree.leaves(out_shape)
    moved = sum(a.size * a.dtype.itemsize for a in (*args, *outs))
    return pl.pallas_call(
        body,
        out_shape=out_shape,
        in_specs=[spec(a) for a in args],
        out_specs=jax.tree.map(spec, out_shape),
        compiler_params=pltpu.CompilerParams(vmem_limit_bytes=VMEM_LIMIT),
        cost_estimate=pl.CostEstimate(flops=flops, bytes_accessed=moved, transcendentals=0),
    )(*args)


def packed(value, rows):
    value = jnp.broadcast_to(value, (rows, EXTRA))
    high = value.astype(jnp.bfloat16).astype(jnp.float32)
    middle = (value - high).astype(jnp.bfloat16).astype(jnp.float32)
    low = value - high - middle
    lane = lax.broadcasted_iota(jnp.int32, (rows, EXTRA), 1)
    parts = jnp.where(lane == 0, high, jnp.where(lane == 1, middle, jnp.where(lane == 2, low, 0.0)))
    return parts.astype(jnp.bfloat16)


def unpacked(values, width):
    return jnp.sum(values[0:1, width:])


def text_units_kernel(values_ref, copies_ref):
    unit, _ = unit_rows(values_ref[...])
    half = jnp.concatenate([unit, unit], axis=0).astype(jnp.bfloat16)
    rows = half.shape[0]
    for k in range(copies_ref.shape[0] // rows):
        copies_ref[k * rows : (k + 1) * rows, :] = half


def image_units_kernel(values_ref, other_ref, half_ref, diagonal_ref):
    first = unit_rows(values_ref[...])[0].astype(jnp.bfloat16)
    second = unit_rows(other_ref[...])[0].astype(jnp.bfloat16)
    half_ref[...] = first
    products = first.astype(jnp.float32) * second.astype(jnp.float32)
    diagonal_ref[...] = jnp.broadcast_to(jnp.sum(products), diagonal_ref.shape)


def join_kernel(side_ref, mine_ref, theirs_ref, joined_ref):
    mine, theirs = mine_ref[...].astype(jnp.float32), theirs_ref[...].astype(jnp.float32)
    first = side_ref[0] == 0
    joined = jnp.concatenate(
        [jnp.where(first, mine, theirs), jnp.where(first, theirs, mine)], axis=0
    ).astype(jnp.bfloat16)
    rows = joined.shape[0]
    for k in range(joined_ref.shape[0] // rows):
        joined_ref[k * rows : (k + 1) * rows, :] = joined


def lines(row):
    return [row[:, k * 128 : (k + 1) * 128] for k in range(row.shape[1] // 128)]


def line(rows):
    return jnp.concatenate([rows[k : k + 1, :] for k in range(rows.shape[0])], axis=1)


def eight(rows):
    zero = jnp.zeros((1, 128), jnp.float32)
    return jnp.concatenate([*rows, *[zero] * (8 - len(rows))], axis=0)


def lse_of(parts):
    peak = functools.reduce(jnp.maximum, [jnp.max(p, axis=0, keepdims=True) for p in parts])
    total = sum(jnp.sum(jnp.exp2(p - peak), axis=0, keepdims=True) for p in parts)
    return peak + jnp.log2(total)


def pieces_lse(pieces):
    peak = jnp.max(pieces, axis=0)
    return peak + jnp.log2(jnp.sum(jnp.exp2(pieces - peak[None]), axis=0))


def pair_lse(a, b):
    peak = jnp.maximum(a, b)
    return peak + jnp.log2(jnp.exp2(a - peak) + jnp.exp2(b - peak))


def stats_kernel(factor_ref, image_ref, own_ref, other_ref, diagonal_ref, row_ref, col_ref):
    factor = factor_ref[0] * LOG2_E
    image, own, other = image_ref[...], own_ref[...], other_ref[...]
    own_lse = lse_of([factor * f32_dot(image, own, LAST)])
    other_lse = lse_of([factor * f32_dot(image, other, LAST)])
    row_lse = lse_of([factor * f32_dot(own, image, LAST), factor * f32_dot(other, image, LAST)])
    message = eight([*lines(row_lse), factor * diagonal_ref[0:1, :]])
    row_ref[...] = jnp.broadcast_to(message[None], row_ref.shape)
    col_ref[...] = eight([*lines(own_lse), *lines(other_lse)])


def pair_columns_kernel(mine_ref, theirs_ref, message_ref):
    mine, theirs = mine_ref[...], theirs_ref[...]
    own = pair_lse(mine[0:3], theirs[3:6])
    other = pair_lse(mine[3:6], theirs[0:3])
    message = jnp.concatenate([own, other, jnp.zeros((2, 128), jnp.float32)], axis=0)
    message_ref[...] = jnp.broadcast_to(message[None], message_ref.shape)


def weights_kernel(
    factor_ref, image_ref, own_ref, other_ref, row_ref, pieces_ref,
    image_out, own_out, other_out, share_ref,
):
    factor = factor_ref[0]
    width = own_ref.shape[1]
    cols = pieces_lse(pieces_ref[...])
    own_lse, other_lse = line(cols[0:3]), line(cols[3:6])
    col_share = jnp.sum(own_lse) + jnp.sum(other_lse)
    row_pieces = row_ref[...]
    rows = pieces_lse(row_pieces)[0:3]
    row_share = jnp.sum(rows) - 2.0 * jnp.max(jnp.sum(row_pieces, axis=0)[3:4])
    share_ref[...] = jnp.broadcast_to(row_share, share_ref.shape)
    row_lse = jnp.concatenate(
        [jnp.transpose(jnp.broadcast_to(rows[k : k + 1, :], (128, 128))) for k in range(3)], axis=0
    )[:, 0:1]
    image = image_ref[...]
    image_sum = None
    for text_ref, col_lse in ((own_ref, own_lse), (other_ref, other_lse)):
        text = text_ref[...]
        logits = (factor * LOG2_E) * f32_dot(image, text, LAST)
        weights = (
            (0.5 * factor) * (jnp.exp2(logits - row_lse) + jnp.exp2(logits - col_lse))
        ).astype(jnp.bfloat16)
        part = jnp.dot(weights, text, preferred_element_type=jnp.float32)
        image_sum = part if image_sum is None else image_sum + part
        text_sum = f32_dot(weights, image, FIRST)
        if text_ref is own_ref:
            own_out[...] = text_sum
        else:
            other_out[:, :width] = text_sum.astype(jnp.bfloat16)
    other_out[:, width:] = packed(row_share, other_out.shape[0])
    image_out[:, :width] = image_sum.astype(jnp.bfloat16)
    image_out[:, width:] = packed(col_share, image_out.shape[0])


def pair_sums_kernel(own_ref, theirs_ref, share_ref, message_ref):
    width = own_ref.shape[1]
    theirs = theirs_ref[...].astype(jnp.float32)
    message_ref[:, :width] = (own_ref[...] + theirs[:, :width]).astype(jnp.bfloat16)
    share = jnp.max(share_ref[...]) + unpacked(theirs, width)
    message_ref[:, width:] = packed(share, message_ref.shape[0])


def slabs_sum(pieces_ref, rows):
    total = None
    for k in range(pieces_ref.shape[0] // (2 * rows)):
        both = pieces_ref[2 * rows * k : 2 * rows * (k + 1), :].astype(jnp.float32)
        both = both[:rows] + both[rows:]
        total = both if total is None else total + both
    return total


def near_sums_kernel(side_ref, pieces_ref, keep_ref, send_ref, share_ref):
    rows, width = keep_ref.shape
    total = slabs_sum(pieces_ref, 2 * rows)
    share = unpacked(total, width)
    first = side_ref[0] == 0
    lower, upper = total[:rows, :width], total[rows:, :width]
    keep_ref[...] = jnp.where(first, lower, upper)
    send_ref[:, :width] = jnp.where(first, upper, lower).astype(jnp.bfloat16)
    send_ref[:, width:] = packed(share, rows)
    share_ref[...] = jnp.broadcast_to(share, share_ref.shape)


def gradient(factor, values, paired, total):
    unit, inverse = unit_rows(values)
    pull = total - factor * unit_rows(paired)[0].astype(jnp.bfloat16).astype(jnp.float32)
    return (pull - unit * jnp.sum(pull * unit, axis=1, keepdims=True)) * inverse


def image_gradient_kernel(
    factor_ref, values_ref, paired_ref, kept_ref, theirs_ref, shared_ref, gradient_ref, share_ref
):
    width = kept_ref.shape[1]
    theirs = theirs_ref[...].astype(jnp.float32)
    total = kept_ref[...] + theirs[:, :width]
    gradient_ref[...] = gradient(factor_ref[0], values_ref[...], paired_ref[...], total)
    share = jnp.max(shared_ref[...]) + unpacked(theirs, width)
    share_ref[...] = jnp.broadcast_to(share, share_ref.shape)


def text_gradient_kernel(
    whole, factor_ref, values_ref, paired_ref, pieces_ref, shared_ref, gradient_ref, loss_ref
):
    rows, width = values_ref.shape
    total = slabs_sum(pieces_ref, rows)
    gradient_ref[...] = gradient(
        factor_ref[0], values_ref[...], paired_ref[...], total[:, :width]
    )
    loss_ref[0] = (jnp.max(shared_ref[...]) + unpacked(total, width)) * (1.0 / (LOG2_E * whole))


def exchanged(blocks, axis):
    count = lax.axis_size(axis)
    split = blocks.reshape(count, -1, blocks.shape[-1])
    return lax.all_to_all(split, axis, split_axis=0, concat_axis=0, tiled=True).reshape(blocks.shape)


def swapped(x, axis):
    return lax.ppermute(x, axis, [(0, 1), (1, 0)])


def after(x, first):
    return lax.optimization_barrier((x, first))[0]


def shape(dims, dtype):
    return jax.ShapeDtypeStruct(dims, dtype)


def place(axis):
    return lax.axis_index(axis).astype(jnp.int32).reshape(1)


def on_device(image_emb, text_emb, factor):
    own_rows, width = image_emb.shape
    inner, chips = lax.axis_size(INNER), lax.axis_size(CHIPS)
    bf16, f32 = jnp.bfloat16, jnp.float32
    image_rows, text_rows = own_rows * inner, own_rows * chips
    wide = width + EXTRA
    work = 2 * image_rows * text_rows * width
    far = place(FAR)
    tile = shape((8, 128), f32)

    text_copies = kernel_call(text_units_kernel, shape((text_rows, width), bf16), text_emb)
    text_own = exchanged(text_copies, CHIPS)
    text_other = swapped(text_own, CORE)
    half, diagonal = kernel_call(
        image_units_kernel, (shape((own_rows, width), bf16), tile), image_emb, text_emb
    )
    image_copies = kernel_call(
        join_kernel, shape((image_rows, width), bf16), far, half, swapped(half, FAR)
    )
    image_group = exchanged(after(image_copies, text_own), NEAR)

    row_message, col_part = kernel_call(
        stats_kernel,
        (shape((inner, 8, 128), f32), tile),
        factor, image_group, text_own, text_other, diagonal,
        flops=4 * work,
    )
    row_pieces = exchanged(row_message, INNER)
    col_message = kernel_call(
        pair_columns_kernel, shape((chips, 8, 128), f32), col_part, swapped(col_part, CORE)
    )
    col_pieces = exchanged(after(col_message, row_pieces), CHIPS)

    image_part, own_part, other_part, row_share = kernel_call(
        weights_kernel,
        (
            shape((image_rows, wide), bf16),
            shape((text_rows, width), f32),
            shape((text_rows, wide), bf16),
            tile,
        ),
        factor, image_group, text_own, text_other, row_pieces, col_pieces,
        flops=6 * work,
    )
    image_pieces = exchanged(image_part, NEAR)
    text_part = kernel_call(
        pair_sums_kernel, shape((text_rows, wide), bf16),
        own_part, swapped(other_part, CORE), row_share,
    )
    text_pieces = exchanged(after(text_part, image_pieces), CHIPS)

    kept, sent, share = kernel_call(
        near_sums_kernel,
        (shape((own_rows, width), f32), shape((own_rows, wide), bf16), tile),
        far, image_pieces,
    )
    out = shape((own_rows, width), f32)
    image_grad, share = kernel_call(
        image_gradient_kernel, (out, tile),
        factor, image_emb, text_emb, kept, swapped(sent, FAR), share,
    )
    whole = 2.0 * own_rows * inner * chips * lax.axis_size(CORE)
    text_grad, mean_loss = kernel_call(
        functools.partial(text_gradient_kernel, whole), (out, shape((1,), f32)),
        factor, text_emb, image_emb, text_pieces, share,
    )
    return (mean_loss, image_grad, text_grad)


def solution(mesh):
    split = Mesh(mesh.devices.reshape(2, 2, 2, 2, 4, 4, 2), ALL)
    in_specs = (P(ALL, None), P(ALL, None), P())
    out_specs = (P(), P(ALL, None), P(ALL, None))
    return jax.shard_map(
        on_device, mesh=split, in_specs=in_specs, out_specs=out_specs, check_vma=False
    )
```

```python
import functools

import jax
import jax.numpy as jnp
from jax import lax
from jax.experimental import pallas as pl
from jax.experimental.pallas import tpu as pltpu
from jax.sharding import Mesh
from jax.sharding import PartitionSpec as P

ALL = ("z0", "y2", "y1", "y0", "x", "zh", "c")
INNER = ("z0", "y2", "y1", "y0")
CHIPS = ("x", "zh")
NEAR = ("z0", "y0")
FAR = ("y2", "y1")
CORE = "c"

EPSILON = 1e-06
LAST = (((1,), (1,)), ((), ()))
FIRST = (((0,), (0,)), ((), ()))
VMEM_LIMIT = 24 * 1024 * 1024
EXTRA = 128
LOG2_E = 1.4426950408889634


def f32_dot(a, b, dims):
    return lax.dot_general(a, b, dims, preferred_element_type=jnp.float32)


def unit_rows(values):
    inverse = lax.rsqrt(jnp.sum(values * values, axis=1, keepdims=True) + EPSILON)
    return values * inverse, inverse


def kernel_call(body, out_shape, *args, flops=0):
    def spec(a):
        return pl.BlockSpec(memory_space=pltpu.SMEM if a.size == 1 else pltpu.VMEM)

    outs = jax.tree.leaves(out_shape)
    moved = sum(a.size * a.dtype.itemsize for a in (*args, *outs))
    return pl.pallas_call(
        body,
        out_shape=out_shape,
        in_specs=[spec(a) for a in args],
        out_specs=jax.tree.map(spec, out_shape),
        compiler_params=pltpu.CompilerParams(vmem_limit_bytes=VMEM_LIMIT),
        cost_estimate=pl.CostEstimate(flops=flops, bytes_accessed=moved, transcendentals=0),
    )(*args)


def packed(value, rows):
    value = jnp.broadcast_to(value, (rows, EXTRA))
    high = value.astype(jnp.bfloat16).astype(jnp.float32)
    middle = (value - high).astype(jnp.bfloat16).astype(jnp.float32)
    low = value - high - middle
    lane = lax.broadcasted_iota(jnp.int32, (rows, EXTRA), 1)
    parts = jnp.where(lane == 0, high, jnp.where(lane == 1, middle, jnp.where(lane == 2, low, 0.0)))
    return parts.astype(jnp.bfloat16)


def unpacked(values, width):
    return jnp.sum(values[0:1, width:])


def text_units_kernel(values_ref, copies_ref):
    unit, _ = unit_rows(values_ref[...])
    half = jnp.concatenate([unit, unit], axis=0).astype(jnp.bfloat16)
    rows = half.shape[0]
    for k in range(copies_ref.shape[0] // rows):
        copies_ref[k * rows : (k + 1) * rows, :] = half


def image_units_kernel(values_ref, other_ref, half_ref, diagonal_ref):
    first = unit_rows(values_ref[...])[0].astype(jnp.bfloat16)
    second = unit_rows(other_ref[...])[0].astype(jnp.bfloat16)
    half_ref[...] = first
    products = first.astype(jnp.float32) * second.astype(jnp.float32)
    diagonal_ref[...] = jnp.broadcast_to(jnp.sum(products), diagonal_ref.shape)


def chosen(number, blocks):
    found = blocks[0]
    for k in range(1, len(blocks)):
        found = jnp.where(number == k, blocks[k], found)
    return found


def join_kernel(place_ref, *refs):
    *block_refs, joined_ref = refs
    blocks = [ref[...].astype(jnp.float32) for ref in block_refs]
    ordered = [chosen(place_ref[0] ^ k, blocks) for k in range(len(blocks))]
    rows = 2 * blocks[0].shape[0]
    for pair in range(len(blocks) // 2):
        half = jnp.concatenate(ordered[2 * pair : 2 * pair + 2], axis=0).astype(jnp.bfloat16)
        for at in range(pair * rows, joined_ref.shape[0], rows * len(blocks) // 2):
            joined_ref[at : at + rows, :] = half


def lines(row):
    return [row[:, k * 128 : (k + 1) * 128] for k in range(row.shape[1] // 128)]


def line(rows):
    return jnp.concatenate([rows[k : k + 1, :] for k in range(rows.shape[0])], axis=1)


def eight(rows):
    zero = jnp.zeros((1, 128), jnp.float32)
    return jnp.concatenate([*rows, *[zero] * (8 - len(rows))], axis=0)


def lse_of(parts):
    peak = functools.reduce(jnp.maximum, [jnp.max(p, axis=0, keepdims=True) for p in parts])
    total = sum(jnp.sum(jnp.exp2(p - peak), axis=0, keepdims=True) for p in parts)
    return peak + jnp.log2(total)


def pieces_lse(pieces):
    peak = jnp.max(pieces, axis=0)
    return peak + jnp.log2(jnp.sum(jnp.exp2(pieces - peak[None]), axis=0))


def pair_lse(a, b):
    peak = jnp.maximum(a, b)
    return peak + jnp.log2(jnp.exp2(a - peak) + jnp.exp2(b - peak))


def stats_kernel(factor_ref, image_ref, own_ref, other_ref, diagonal_ref, row_ref, col_ref):
    factor = factor_ref[0] * LOG2_E
    image, own, other = image_ref[...], own_ref[...], other_ref[...]
    own_lse = lse_of([factor * f32_dot(image, own, LAST)])
    other_lse = lse_of([factor * f32_dot(image, other, LAST)])
    row_lse = lse_of([factor * f32_dot(own, image, LAST), factor * f32_dot(other, image, LAST)])
    message = eight([*lines(row_lse), factor * diagonal_ref[0:1, :]])
    row_ref[...] = jnp.broadcast_to(message[None], row_ref.shape)
    col_ref[...] = eight([*lines(own_lse), *lines(other_lse)])


def pair_columns_kernel(mine_ref, theirs_ref, message_ref):
    mine, theirs = mine_ref[...], theirs_ref[...]
    own = pair_lse(mine[0:3], theirs[3:6])
    other = pair_lse(mine[3:6], theirs[0:3])
    message = jnp.concatenate([own, other, jnp.zeros((2, 128), jnp.float32)], axis=0)
    message_ref[...] = jnp.broadcast_to(message[None], message_ref.shape)


def weights_kernel(
    factor_ref, image_ref, own_ref, other_ref, row_ref, pieces_ref,
    image_out, own_out, other_out, share_ref,
):
    factor = factor_ref[0]
    width = own_ref.shape[1]
    cols = pieces_lse(pieces_ref[...])
    own_lse, other_lse = line(cols[0:3]), line(cols[3:6])
    col_share = jnp.sum(own_lse) + jnp.sum(other_lse)
    row_pieces = row_ref[...]
    rows = pieces_lse(row_pieces)[0:3]
    row_share = jnp.sum(rows) - 2.0 * jnp.max(jnp.sum(row_pieces, axis=0)[3:4])
    share_ref[...] = jnp.broadcast_to(row_share, share_ref.shape)
    row_lse = jnp.concatenate(
        [jnp.transpose(jnp.broadcast_to(rows[k : k + 1, :], (128, 128))) for k in range(3)], axis=0
    )[:, 0:1]
    image = image_ref[...]
    image_sum = None
    for text_ref, col_lse in ((own_ref, own_lse), (other_ref, other_lse)):
        text = text_ref[...]
        logits = (factor * LOG2_E) * f32_dot(image, text, LAST)
        weights = (
            (0.5 * factor) * (jnp.exp2(logits - row_lse) + jnp.exp2(logits - col_lse))
        ).astype(jnp.bfloat16)
        part = jnp.dot(weights, text, preferred_element_type=jnp.float32)
        image_sum = part if image_sum is None else image_sum + part
        text_sum = f32_dot(weights, image, FIRST)
        if text_ref is own_ref:
            own_out[...] = text_sum
        else:
            other_out[:, :width] = text_sum.astype(jnp.bfloat16)
    other_out[:, width:] = packed(row_share, other_out.shape[0])
    image_out[:, :width] = image_sum.astype(jnp.bfloat16)
    image_out[:, width:] = packed(col_share, image_out.shape[0])


def pair_sums_kernel(own_ref, theirs_ref, share_ref, message_ref):
    width = own_ref.shape[1]
    theirs = theirs_ref[...].astype(jnp.float32)
    message_ref[:, :width] = (own_ref[...] + theirs[:, :width]).astype(jnp.bfloat16)
    share = jnp.max(share_ref[...]) + unpacked(theirs, width)
    message_ref[:, width:] = packed(share, message_ref.shape[0])


def slabs_sum(pieces_ref, rows):
    total = None
    for k in range(pieces_ref.shape[0] // (2 * rows)):
        both = pieces_ref[2 * rows * k : 2 * rows * (k + 1), :].astype(jnp.float32)
        both = both[:rows] + both[rows:]
        total = both if total is None else total + both
    return total


def near_sums_kernel(place_ref, pieces_ref, keep_ref, *refs):
    *send_refs, share_ref = refs
    rows, width = keep_ref.shape
    count = len(send_refs) + 1
    total = slabs_sum(pieces_ref, count * rows)
    share = unpacked(total, width)
    blocks = [total[k * rows : (k + 1) * rows, :width] for k in range(count)]
    keep_ref[...] = chosen(place_ref[0], blocks)
    for k, send_ref in enumerate(send_refs):
        send_ref[:, :width] = chosen(place_ref[0] ^ (k + 1), blocks).astype(jnp.bfloat16)
        send_ref[:, width:] = packed(share, rows)
    share_ref[...] = jnp.broadcast_to(share, share_ref.shape)


def gradient(factor, values, paired, total):
    unit, inverse = unit_rows(values)
    pull = total - factor * unit_rows(paired)[0].astype(jnp.bfloat16).astype(jnp.float32)
    return (pull - unit * jnp.sum(pull * unit, axis=1, keepdims=True)) * inverse


def image_gradient_kernel(
    factor_ref, values_ref, paired_ref, kept_ref, shared_ref, first_ref, second_ref, third_ref,
    gradient_ref, share_ref,
):
    width = kept_ref.shape[1]
    first, second, third = (
        ref[...].astype(jnp.float32) for ref in (first_ref, second_ref, third_ref)
    )
    total = (kept_ref[...] + first[:, :width]) + (second[:, :width] + third[:, :width])
    gradient_ref[...] = gradient(factor_ref[0], values_ref[...], paired_ref[...], total)
    share = (jnp.max(shared_ref[...]) + unpacked(first, width)) + (
        unpacked(second, width) + unpacked(third, width)
    )
    share_ref[...] = jnp.broadcast_to(share, share_ref.shape)


def text_gradient_kernel(
    whole, factor_ref, values_ref, paired_ref, pieces_ref, shared_ref, gradient_ref, loss_ref
):
    rows, width = values_ref.shape
    total = slabs_sum(pieces_ref, rows)
    gradient_ref[...] = gradient(
        factor_ref[0], values_ref[...], paired_ref[...], total[:, :width]
    )
    loss_ref[0] = (jnp.max(shared_ref[...]) + unpacked(total, width)) * (1.0 / (LOG2_E * whole))


def exchanged(blocks, axis):
    count = lax.axis_size(axis)
    split = blocks.reshape(count, -1, blocks.shape[-1])
    return lax.all_to_all(split, axis, split_axis=0, concat_axis=0, tiled=True).reshape(blocks.shape)


def swapped(x, axis, offset=1):
    return lax.ppermute(x, axis, [(k, k ^ offset) for k in range(lax.axis_size(axis))])


def after(x, first):
    return lax.optimization_barrier((x, first))[0]


def shape(dims, dtype):
    return jax.ShapeDtypeStruct(dims, dtype)


def place(axis):
    return lax.axis_index(axis).astype(jnp.int32).reshape(1)


def on_device(image_emb, text_emb, factor):
    own_rows, width = image_emb.shape
    inner, chips = lax.axis_size(INNER), lax.axis_size(CHIPS)
    bf16, f32 = jnp.bfloat16, jnp.float32
    image_rows, text_rows = own_rows * inner, own_rows * chips
    wide = width + EXTRA
    work = 2 * image_rows * text_rows * width
    far, fars = place(FAR), lax.axis_size(FAR)
    tile = shape((8, 128), f32)

    text_copies = kernel_call(text_units_kernel, shape((text_rows, width), bf16), text_emb)
    text_own = exchanged(text_copies, CHIPS)
    text_other = swapped(text_own, CORE)
    half, diagonal = kernel_call(
        image_units_kernel, (shape((own_rows, width), bf16), tile), image_emb, text_emb
    )
    image_copies = kernel_call(
        join_kernel, shape((image_rows, width), bf16),
        far, half, *(swapped(half, FAR, k) for k in range(1, fars)),
    )
    image_group = exchanged(after(image_copies, text_own), NEAR)

    row_message, col_part = kernel_call(
        stats_kernel,
        (shape((inner, 8, 128), f32), tile),
        factor, image_group, text_own, text_other, diagonal,
        flops=4 * work,
    )
    row_pieces = exchanged(row_message, INNER)
    col_message = kernel_call(
        pair_columns_kernel, shape((chips, 8, 128), f32), col_part, swapped(col_part, CORE)
    )
    col_pieces = exchanged(after(col_message, row_pieces), CHIPS)

    image_part, own_part, other_part, row_share = kernel_call(
        weights_kernel,
        (
            shape((image_rows, wide), bf16),
            shape((text_rows, width), f32),
            shape((text_rows, wide), bf16),
            tile,
        ),
        factor, image_group, text_own, text_other, row_pieces, col_pieces,
        flops=6 * work,
    )
    image_pieces = exchanged(image_part, NEAR)
    text_part = kernel_call(
        pair_sums_kernel, shape((text_rows, wide), bf16),
        own_part, swapped(other_part, CORE), row_share,
    )
    text_pieces = exchanged(after(text_part, image_pieces), CHIPS)

    sent = [shape((own_rows, wide), bf16)] * (fars - 1)
    kept, *sent, share = kernel_call(
        near_sums_kernel, (shape((own_rows, width), f32), *sent, tile), far, image_pieces
    )
    out = shape((own_rows, width), f32)
    image_grad, share = kernel_call(
        image_gradient_kernel, (out, tile),
        factor, image_emb, text_emb, kept, share,
        *(swapped(block, FAR, k + 1) for k, block in enumerate(sent)),
    )
    whole = 2.0 * own_rows * inner * chips * lax.axis_size(CORE)
    text_grad, mean_loss = kernel_call(
        functools.partial(text_gradient_kernel, whole), (out, shape((1,), f32)),
        factor, text_emb, image_emb, text_pieces, share,
    )
    return (mean_loss, image_grad, text_grad)


def solution(mesh):
    split = Mesh(mesh.devices.reshape(2, 2, 2, 2, 4, 4, 2), ALL)
    in_specs = (P(ALL, None), P(ALL, None), P())
    out_specs = (P(), P(ALL, None), P(ALL, None))
    return jax.shard_map(
        on_device, mesh=split, in_specs=in_specs, out_specs=out_specs, check_vma=False
    )
```

```python
import functools

import jax
import jax.numpy as jnp
from jax import lax
from jax.experimental import pallas as pl
from jax.experimental.pallas import tpu as pltpu
from jax.sharding import Mesh
from jax.sharding import PartitionSpec as P

ALL = ("z0", "y2", "y1", "y0", "x", "zh", "c")
INNER = ("z0", "y2", "y1", "y0")
CHIPS = ("x", "zh")
NEAR = ("z0", "y0")
FAR = ("y2", "y1")
CORE = "c"

EPSILON = 1e-06
LAST = (((1,), (1,)), ((), ()))
FIRST = (((0,), (0,)), ((), ()))
VMEM_LIMIT = 24 * 1024 * 1024
EXTRA = 128
LOG2_E = 1.4426950408889634


def f32_dot(a, b, dims):
    return lax.dot_general(a, b, dims, preferred_element_type=jnp.float32)


def unit_rows(values):
    inverse = lax.rsqrt(jnp.sum(values * values, axis=1, keepdims=True) + EPSILON)
    return values * inverse, inverse


def kernel_call(body, out_shape, *args, flops=0):
    def spec(a):
        return pl.BlockSpec(memory_space=pltpu.SMEM if a.size == 1 else pltpu.VMEM)

    outs = jax.tree.leaves(out_shape)
    moved = sum(a.size * a.dtype.itemsize for a in (*args, *outs))
    return pl.pallas_call(
        body,
        out_shape=out_shape,
        in_specs=[spec(a) for a in args],
        out_specs=jax.tree.map(spec, out_shape),
        compiler_params=pltpu.CompilerParams(vmem_limit_bytes=VMEM_LIMIT),
        cost_estimate=pl.CostEstimate(flops=flops, bytes_accessed=moved, transcendentals=0),
    )(*args)


def packed(value, rows):
    value = jnp.broadcast_to(value, (rows, EXTRA))
    high = value.astype(jnp.bfloat16).astype(jnp.float32)
    middle = (value - high).astype(jnp.bfloat16).astype(jnp.float32)
    low = value - high - middle
    lane = lax.broadcasted_iota(jnp.int32, (rows, EXTRA), 1)
    parts = jnp.where(lane == 0, high, jnp.where(lane == 1, middle, jnp.where(lane == 2, low, 0.0)))
    return parts.astype(jnp.bfloat16)


def unpacked(values, width):
    return jnp.sum(values[0:1, width:])


def text_units_kernel(values_ref, copies_ref):
    unit, _ = unit_rows(values_ref[...])
    half = jnp.concatenate([unit, unit], axis=0).astype(jnp.bfloat16)
    rows = half.shape[0]
    for k in range(copies_ref.shape[0] // rows):
        copies_ref[k * rows : (k + 1) * rows, :] = half


def image_units_kernel(values_ref, other_ref, half_ref, diagonal_ref):
    first = unit_rows(values_ref[...])[0].astype(jnp.bfloat16)
    second = unit_rows(other_ref[...])[0].astype(jnp.bfloat16)
    half_ref[...] = first
    products = first.astype(jnp.float32) * second.astype(jnp.float32)
    diagonal_ref[...] = jnp.broadcast_to(jnp.sum(products), diagonal_ref.shape)


def chosen(number, blocks):
    found = blocks[0]
    for k in range(1, len(blocks)):
        found = jnp.where(number == k, blocks[k], found)
    return found


def join_kernel(place_ref, *refs):
    *block_refs, joined_ref = refs
    blocks = [ref[...].astype(jnp.float32) for ref in block_refs]
    ordered = [chosen(place_ref[0] ^ k, blocks) for k in range(len(blocks))]
    rows = 2 * blocks[0].shape[0]
    for pair in range(len(blocks) // 2):
        half = jnp.concatenate(ordered[2 * pair : 2 * pair + 2], axis=0).astype(jnp.bfloat16)
        for at in range(pair * rows, joined_ref.shape[0], rows * len(blocks) // 2):
            joined_ref[at : at + rows, :] = half


def lines(row):
    return [row[:, k * 128 : (k + 1) * 128] for k in range(row.shape[1] // 128)]


def line(rows):
    return jnp.concatenate([rows[k : k + 1, :] for k in range(rows.shape[0])], axis=1)


def eight(rows):
    zero = jnp.zeros((1, 128), jnp.float32)
    return jnp.concatenate([*rows, *[zero] * (8 - len(rows))], axis=0)


def lse_of(parts):
    peak = functools.reduce(jnp.maximum, [jnp.max(p, axis=0, keepdims=True) for p in parts])
    total = sum(jnp.sum(jnp.exp2(p - peak), axis=0, keepdims=True) for p in parts)
    return peak + jnp.log2(total)


def pieces_lse(pieces):
    peak = jnp.max(pieces, axis=0)
    return peak + jnp.log2(jnp.sum(jnp.exp2(pieces - peak[None]), axis=0))


def pair_lse(a, b):
    peak = jnp.maximum(a, b)
    return peak + jnp.log2(jnp.exp2(a - peak) + jnp.exp2(b - peak))


def rows_kernel(factor_ref, image_ref, own_ref, other_ref, diagonal_ref, message_ref):
    factor = factor_ref[0] * LOG2_E
    image = image_ref[...]
    lse = lse_of([factor * f32_dot(text[...], image, LAST) for text in (own_ref, other_ref)])
    message = eight([*lines(lse), factor * diagonal_ref[0:1, :]])
    message_ref[...] = jnp.broadcast_to(message[None], message_ref.shape)


def columns_kernel(factor_ref, image_ref, own_ref, other_ref, message_ref):
    factor = factor_ref[0] * LOG2_E
    image = image_ref[...]
    own, other = (
        lse_of([factor * f32_dot(image, text[...], LAST)]) for text in (own_ref, other_ref)
    )
    message_ref[...] = eight([*lines(own), *lines(other)])


def pair_columns_kernel(mine_ref, theirs_ref, message_ref):
    mine, theirs = mine_ref[...], theirs_ref[...]
    own = pair_lse(mine[0:3], theirs[3:6])
    other = pair_lse(mine[3:6], theirs[0:3])
    message = jnp.concatenate([own, other, jnp.zeros((2, 128), jnp.float32)], axis=0)
    message_ref[...] = jnp.broadcast_to(message[None], message_ref.shape)


def weights_kernel(
    factor_ref, image_ref, own_ref, other_ref, row_ref, pieces_ref,
    image_out, own_out, other_out, share_ref,
):
    factor = factor_ref[0]
    width = own_ref.shape[1]
    cols = pieces_lse(pieces_ref[...])
    own_lse, other_lse = line(cols[0:3]), line(cols[3:6])
    col_share = jnp.sum(own_lse) + jnp.sum(other_lse)
    row_pieces = row_ref[...]
    rows = pieces_lse(row_pieces)[0:3]
    row_share = jnp.sum(rows) - 2.0 * jnp.max(jnp.sum(row_pieces, axis=0)[3:4])
    share_ref[...] = jnp.broadcast_to(row_share, share_ref.shape)
    row_lse = jnp.concatenate(
        [jnp.transpose(jnp.broadcast_to(rows[k : k + 1, :], (128, 128))) for k in range(3)], axis=0
    )[:, 0:1]
    image = image_ref[...]
    sums = []
    for text_ref, weights_ref, col_lse in (
        (own_ref, own_out, own_lse), (other_ref, other_out, other_lse)
    ):
        text = text_ref[...]
        logits = (factor * LOG2_E) * f32_dot(image, text, LAST)
        weights = (
            (0.5 * factor) * (jnp.exp2(logits - row_lse) + jnp.exp2(logits - col_lse))
        ).astype(jnp.bfloat16)
        weights_ref[...] = weights
        sums.append(jnp.dot(weights, text, preferred_element_type=jnp.float32))
    image_out[:, :width] = (sums[0] + sums[1]).astype(jnp.bfloat16)
    image_out[:, width:] = packed(col_share, image_out.shape[0])


def text_sums_kernel(image_ref, own_ref, other_ref, share_ref, own_out, other_out):
    image = image_ref[...]
    width = image.shape[1]
    other_out[:, :width] = f32_dot(other_ref[...], image, FIRST).astype(jnp.bfloat16)
    other_out[:, width:] = packed(jnp.max(share_ref[...]), other_out.shape[0])
    own_out[...] = f32_dot(own_ref[...], image, FIRST)


def pair_sums_kernel(own_ref, theirs_ref, share_ref, message_ref):
    width = own_ref.shape[1]
    theirs = theirs_ref[...].astype(jnp.float32)
    message_ref[:, :width] = (own_ref[...] + theirs[:, :width]).astype(jnp.bfloat16)
    share = jnp.max(share_ref[...]) + unpacked(theirs, width)
    message_ref[:, width:] = packed(share, message_ref.shape[0])


def slabs_sum(pieces_ref, rows):
    total = None
    for k in range(pieces_ref.shape[0] // (2 * rows)):
        both = pieces_ref[2 * rows * k : 2 * rows * (k + 1), :].astype(jnp.float32)
        both = both[:rows] + both[rows:]
        total = both if total is None else total + both
    return total


def near_sums_kernel(place_ref, pieces_ref, keep_ref, *refs):
    *send_refs, share_ref = refs
    rows, width = keep_ref.shape
    count = len(send_refs) + 1
    total = slabs_sum(pieces_ref, count * rows)
    share = unpacked(total, width)
    blocks = [total[k * rows : (k + 1) * rows, :width] for k in range(count)]
    keep_ref[...] = chosen(place_ref[0], blocks)
    for k, send_ref in enumerate(send_refs):
        send_ref[:, :width] = chosen(place_ref[0] ^ (k + 1), blocks).astype(jnp.bfloat16)
        send_ref[:, width:] = packed(share, rows)
    share_ref[...] = jnp.broadcast_to(share, share_ref.shape)


def gradient(factor, values, paired, total):
    unit, inverse = unit_rows(values)
    pull = total - factor * unit_rows(paired)[0].astype(jnp.bfloat16).astype(jnp.float32)
    return (pull - unit * jnp.sum(pull * unit, axis=1, keepdims=True)) * inverse


def image_gradient_kernel(
    factor_ref, values_ref, paired_ref, kept_ref, shared_ref, first_ref, second_ref, third_ref,
    gradient_ref, share_ref,
):
    width = kept_ref.shape[1]
    first, second, third = (
        ref[...].astype(jnp.float32) for ref in (first_ref, second_ref, third_ref)
    )
    total = (kept_ref[...] + first[:, :width]) + (second[:, :width] + third[:, :width])
    gradient_ref[...] = gradient(factor_ref[0], values_ref[...], paired_ref[...], total)
    share = (jnp.max(shared_ref[...]) + unpacked(first, width)) + (
        unpacked(second, width) + unpacked(third, width)
    )
    share_ref[...] = jnp.broadcast_to(share, share_ref.shape)


def text_gradient_kernel(
    whole, factor_ref, values_ref, paired_ref, pieces_ref, shared_ref, gradient_ref, loss_ref
):
    rows, width = values_ref.shape
    total = slabs_sum(pieces_ref, rows)
    gradient_ref[...] = gradient(
        factor_ref[0], values_ref[...], paired_ref[...], total[:, :width]
    )
    loss_ref[0] = (jnp.max(shared_ref[...]) + unpacked(total, width)) * (1.0 / (LOG2_E * whole))


def exchanged(blocks, axis):
    count = lax.axis_size(axis)
    split = blocks.reshape(count, -1, blocks.shape[-1])
    return lax.all_to_all(split, axis, split_axis=0, concat_axis=0, tiled=True).reshape(blocks.shape)


def swapped(x, axis, offset=1):
    return lax.ppermute(x, axis, [(k, k ^ offset) for k in range(lax.axis_size(axis))])


def after(x, first):
    return lax.optimization_barrier((x, first))[0]


def shape(dims, dtype):
    return jax.ShapeDtypeStruct(dims, dtype)


def place(axis):
    return lax.axis_index(axis).astype(jnp.int32).reshape(1)


def on_device(image_emb, text_emb, factor):
    own_rows, width = image_emb.shape
    inner, chips = lax.axis_size(INNER), lax.axis_size(CHIPS)
    bf16, f32 = jnp.bfloat16, jnp.float32
    image_rows, text_rows = own_rows * inner, own_rows * chips
    wide = width + EXTRA
    work = 2 * image_rows * text_rows * width
    far, fars = place(FAR), lax.axis_size(FAR)
    tile = shape((8, 128), f32)

    text_copies = kernel_call(text_units_kernel, shape((text_rows, width), bf16), text_emb)
    text_own = exchanged(text_copies, CHIPS)
    text_other = swapped(text_own, CORE)
    half, diagonal = kernel_call(
        image_units_kernel, (shape((own_rows, width), bf16), tile), image_emb, text_emb
    )
    image_copies = kernel_call(
        join_kernel, shape((image_rows, width), bf16),
        far, half, *(swapped(half, FAR, k) for k in range(1, fars)),
    )
    image_group = exchanged(after(image_copies, text_own), NEAR)

    tile_of = (factor, image_group, text_own, text_other)
    row_message = kernel_call(
        rows_kernel, shape((inner, 8, 128), f32), *tile_of, diagonal, flops=2 * work
    )
    row_pieces = exchanged(row_message, INNER)
    col_part = kernel_call(columns_kernel, tile, *tile_of, flops=2 * work)
    col_message = kernel_call(
        pair_columns_kernel, shape((chips, 8, 128), f32), col_part, swapped(col_part, CORE)
    )
    col_pieces = exchanged(after(col_message, row_pieces), CHIPS)

    half_tile = shape((image_rows, text_rows), bf16)
    image_part, *weights, row_share = kernel_call(
        weights_kernel,
        (shape((image_rows, wide), bf16), half_tile, half_tile, tile),
        *tile_of, row_pieces, col_pieces,
        flops=4 * work,
    )
    own_part, other_part = kernel_call(
        text_sums_kernel,
        (shape((text_rows, width), f32), shape((text_rows, wide), bf16)),
        image_group, *weights, row_share,
        flops=2 * work,
    )
    image_pieces = exchanged(image_part, NEAR)
    text_part = kernel_call(
        pair_sums_kernel, shape((text_rows, wide), bf16),
        own_part, swapped(other_part, CORE), row_share,
    )
    text_pieces = exchanged(after(text_part, image_pieces), CHIPS)

    sent = [shape((own_rows, wide), bf16)] * (fars - 1)
    kept, *sent, share = kernel_call(
        near_sums_kernel, (shape((own_rows, width), f32), *sent, tile), far, image_pieces
    )
    out = shape((own_rows, width), f32)
    image_grad, share = kernel_call(
        image_gradient_kernel, (out, tile),
        factor, image_emb, text_emb, kept, share,
        *(swapped(block, FAR, k + 1) for k, block in enumerate(sent)),
    )
    whole = 2.0 * own_rows * inner * chips * lax.axis_size(CORE)
    text_grad, mean_loss = kernel_call(
        functools.partial(text_gradient_kernel, whole), (out, shape((1,), f32)),
        factor, text_emb, image_emb, text_pieces, share,
    )
    return (mean_loss, image_grad, text_grad)


def solution(mesh):
    split = Mesh(mesh.devices.reshape(2, 2, 2, 2, 4, 4, 2), ALL)
    in_specs = (P(ALL, None), P(ALL, None), P())
    out_specs = (P(), P(ALL, None), P(ALL, None))
    return jax.shard_map(
        on_device, mesh=split, in_specs=in_specs, out_specs=out_specs, check_vma=False
    )
```

```python
import functools

import jax
import jax.numpy as jnp
from jax import lax
from jax.experimental import pallas as pl
from jax.experimental.pallas import tpu as pltpu
from jax.sharding import Mesh
from jax.sharding import PartitionSpec as P

ALL = ("z0", "y2", "y1", "y0", "x", "z2", "z1", "c")
INNER = ("y2", "y1", "z2", "z1")
CHIPS = ("x", "y0", "z0")
NEAR = ("y2", "y1", "z1")
FAR = "z2"
CORE = "c"

EPSILON = 1e-06
LAST = (((1,), (1,)), ((), ()))
FIRST = (((0,), (0,)), ((), ()))
VMEM_LIMIT = 24 * 1024 * 1024
EXTRA = 128
LOG2_E = 1.4426950408889634


def f32_dot(a, b, dims):
    return lax.dot_general(a, b, dims, preferred_element_type=jnp.float32)


def unit_rows(values):
    inverse = lax.rsqrt(jnp.sum(values * values, axis=1, keepdims=True) + EPSILON)
    return values * inverse, inverse


def kernel_call(body, out_shape, *args, flops=0):
    def spec(a):
        return pl.BlockSpec(memory_space=pltpu.SMEM if a.size == 1 else pltpu.VMEM)

    outs = jax.tree.leaves(out_shape)
    moved = sum(a.size * a.dtype.itemsize for a in (*args, *outs))
    return pl.pallas_call(
        body,
        out_shape=out_shape,
        in_specs=[spec(a) for a in args],
        out_specs=jax.tree.map(spec, out_shape),
        compiler_params=pltpu.CompilerParams(vmem_limit_bytes=VMEM_LIMIT),
        cost_estimate=pl.CostEstimate(flops=flops, bytes_accessed=moved, transcendentals=0),
    )(*args)


def packed(value, rows):
    value = jnp.broadcast_to(value, (rows, EXTRA))
    high = value.astype(jnp.bfloat16).astype(jnp.float32)
    middle = (value - high).astype(jnp.bfloat16).astype(jnp.float32)
    low = value - high - middle
    lane = lax.broadcasted_iota(jnp.int32, (rows, EXTRA), 1)
    parts = jnp.where(lane == 0, high, jnp.where(lane == 1, middle, jnp.where(lane == 2, low, 0.0)))
    return parts.astype(jnp.bfloat16)


def unpacked(values, width):
    return jnp.sum(values[0:1, width:])


def text_units_kernel(values_ref, copies_ref):
    unit, _ = unit_rows(values_ref[...])
    half = jnp.concatenate([unit, unit], axis=0).astype(jnp.bfloat16)
    rows = half.shape[0]
    for k in range(copies_ref.shape[0] // rows):
        copies_ref[k * rows : (k + 1) * rows, :] = half


def image_units_kernel(values_ref, other_ref, half_ref, diagonal_ref):
    first = unit_rows(values_ref[...])[0].astype(jnp.bfloat16)
    second = unit_rows(other_ref[...])[0].astype(jnp.bfloat16)
    half_ref[...] = first
    products = first.astype(jnp.float32) * second.astype(jnp.float32)
    diagonal_ref[...] = jnp.broadcast_to(jnp.sum(products), diagonal_ref.shape)


def chosen(number, blocks):
    found = blocks[0]
    for k in range(1, len(blocks)):
        found = jnp.where(number == k, blocks[k], found)
    return found


def join_kernel(place_ref, *refs):
    *block_refs, joined_ref = refs
    blocks = [ref[...].astype(jnp.float32) for ref in block_refs]
    ordered = [chosen(place_ref[0] ^ k, blocks) for k in range(len(blocks))]
    rows = 2 * blocks[0].shape[0]
    for pair in range(len(blocks) // 2):
        half = jnp.concatenate(ordered[2 * pair : 2 * pair + 2], axis=0).astype(jnp.bfloat16)
        for at in range(pair * rows, joined_ref.shape[0], rows * len(blocks) // 2):
            joined_ref[at : at + rows, :] = half


def lines(row):
    return [row[:, k * 128 : (k + 1) * 128] for k in range(row.shape[1] // 128)]


def line(rows):
    return jnp.concatenate([rows[k : k + 1, :] for k in range(rows.shape[0])], axis=1)


def eight(rows):
    zero = jnp.zeros((1, 128), jnp.float32)
    return jnp.concatenate([*rows, *[zero] * (8 - len(rows))], axis=0)


def lse_of(parts):
    peak = functools.reduce(jnp.maximum, [jnp.max(p, axis=0, keepdims=True) for p in parts])
    total = sum(jnp.sum(jnp.exp2(p - peak), axis=0, keepdims=True) for p in parts)
    return peak + jnp.log2(total)


def pieces_lse(pieces):
    peak = jnp.max(pieces, axis=0)
    return peak + jnp.log2(jnp.sum(jnp.exp2(pieces - peak[None]), axis=0))


def pair_lse(a, b):
    peak = jnp.maximum(a, b)
    return peak + jnp.log2(jnp.exp2(a - peak) + jnp.exp2(b - peak))


def rows_kernel(factor_ref, image_ref, own_ref, other_ref, diagonal_ref, message_ref):
    factor = factor_ref[0] * LOG2_E
    image = image_ref[...]
    lse = lse_of([factor * f32_dot(text[...], image, LAST) for text in (own_ref, other_ref)])
    message = eight([*lines(lse), factor * diagonal_ref[0:1, :]])
    message_ref[...] = jnp.broadcast_to(message[None], message_ref.shape)


def columns_kernel(factor_ref, image_ref, own_ref, other_ref, message_ref):
    factor = factor_ref[0] * LOG2_E
    image = image_ref[...]
    own, other = (
        lse_of([factor * f32_dot(image, text[...], LAST)]) for text in (own_ref, other_ref)
    )
    message_ref[...] = eight([*lines(own), *lines(other)])


def pair_columns_kernel(mine_ref, theirs_ref, message_ref):
    mine, theirs = mine_ref[...], theirs_ref[...]
    own = pair_lse(mine[0:3], theirs[3:6])
    other = pair_lse(mine[3:6], theirs[0:3])
    message = jnp.concatenate([own, other, jnp.zeros((2, 128), jnp.float32)], axis=0)
    message_ref[...] = jnp.broadcast_to(message[None], message_ref.shape)


def weights_kernel(
    factor_ref, image_ref, own_ref, other_ref, row_ref, pieces_ref,
    image_out, own_out, other_out, share_ref,
):
    factor = factor_ref[0]
    width = own_ref.shape[1]
    cols = pieces_lse(pieces_ref[...])
    own_lse, other_lse = line(cols[0:3]), line(cols[3:6])
    col_share = jnp.sum(own_lse) + jnp.sum(other_lse)
    row_pieces = row_ref[...]
    rows = pieces_lse(row_pieces)[0:3]
    row_share = jnp.sum(rows) - 2.0 * jnp.max(jnp.sum(row_pieces, axis=0)[3:4])
    share_ref[...] = jnp.broadcast_to(row_share, share_ref.shape)
    row_lse = jnp.concatenate(
        [jnp.transpose(jnp.broadcast_to(rows[k : k + 1, :], (128, 128))) for k in range(3)], axis=0
    )[:, 0:1]
    image = image_ref[...]
    sums = []
    for text_ref, weights_ref, col_lse in (
        (own_ref, own_out, own_lse), (other_ref, other_out, other_lse)
    ):
        text = text_ref[...]
        logits = (factor * LOG2_E) * f32_dot(image, text, LAST)
        weights = (
            (0.5 * factor) * (jnp.exp2(logits - row_lse) + jnp.exp2(logits - col_lse))
        ).astype(jnp.bfloat16)
        weights_ref[...] = weights
        sums.append(jnp.dot(weights, text, preferred_element_type=jnp.float32))
    image_out[:, :width] = (sums[0] + sums[1]).astype(jnp.bfloat16)
    image_out[:, width:] = packed(col_share, image_out.shape[0])


def text_sums_kernel(image_ref, own_ref, other_ref, share_ref, own_out, other_out):
    image = image_ref[...]
    width = image.shape[1]
    other_out[:, :width] = f32_dot(other_ref[...], image, FIRST).astype(jnp.bfloat16)
    other_out[:, width:] = packed(jnp.max(share_ref[...]), other_out.shape[0])
    own_out[...] = f32_dot(own_ref[...], image, FIRST)


def pair_sums_kernel(own_ref, theirs_ref, share_ref, message_ref):
    width = own_ref.shape[1]
    theirs = theirs_ref[...].astype(jnp.float32)
    message_ref[:, :width] = (own_ref[...] + theirs[:, :width]).astype(jnp.bfloat16)
    share = jnp.max(share_ref[...]) + unpacked(theirs, width)
    message_ref[:, width:] = packed(share, message_ref.shape[0])


def slabs_sum(pieces_ref, rows):
    total = None
    for k in range(pieces_ref.shape[0] // (2 * rows)):
        both = pieces_ref[2 * rows * k : 2 * rows * (k + 1), :].astype(jnp.float32)
        both = both[:rows] + both[rows:]
        total = both if total is None else total + both
    return total


def near_sums_kernel(place_ref, pieces_ref, keep_ref, *refs):
    *send_refs, share_ref = refs
    rows, width = keep_ref.shape
    count = len(send_refs) + 1
    total = slabs_sum(pieces_ref, count * rows)
    share = unpacked(total, width)
    blocks = [total[k * rows : (k + 1) * rows, :width] for k in range(count)]
    keep_ref[...] = chosen(place_ref[0], blocks)
    for k, send_ref in enumerate(send_refs):
        send_ref[:, :width] = chosen(place_ref[0] ^ (k + 1), blocks).astype(jnp.bfloat16)
        send_ref[:, width:] = packed(share, rows)
    share_ref[...] = jnp.broadcast_to(share, share_ref.shape)


def gradient(factor, values, paired, total):
    unit, inverse = unit_rows(values)
    pull = total - factor * unit_rows(paired)[0].astype(jnp.bfloat16).astype(jnp.float32)
    return (pull - unit * jnp.sum(pull * unit, axis=1, keepdims=True)) * inverse


def tree_sum(terms):
    while len(terms) > 1:
        terms = [a + b for a, b in zip(terms[::2], terms[1::2])]
    return terms[0]


def image_gradient_kernel(factor_ref, values_ref, paired_ref, kept_ref, shared_ref, *refs):
    *far_refs, gradient_ref, share_ref = refs
    width = kept_ref.shape[1]
    fars = [ref[...].astype(jnp.float32) for ref in far_refs]
    total = tree_sum([kept_ref[...]] + [far[:, :width] for far in fars])
    gradient_ref[...] = gradient(factor_ref[0], values_ref[...], paired_ref[...], total)
    share = tree_sum([jnp.max(shared_ref[...])] + [unpacked(far, width) for far in fars])
    share_ref[...] = jnp.broadcast_to(share, share_ref.shape)


def text_gradient_kernel(
    whole, factor_ref, values_ref, paired_ref, pieces_ref, shared_ref, gradient_ref, loss_ref
):
    rows, width = values_ref.shape
    total = slabs_sum(pieces_ref, rows)
    gradient_ref[...] = gradient(
        factor_ref[0], values_ref[...], paired_ref[...], total[:, :width]
    )
    loss_ref[0] = (jnp.max(shared_ref[...]) + unpacked(total, width)) * (1.0 / (LOG2_E * whole))


def exchanged(blocks, axis):
    count = lax.axis_size(axis)
    split = blocks.reshape(count, -1, blocks.shape[-1])
    return lax.all_to_all(split, axis, split_axis=0, concat_axis=0, tiled=True).reshape(blocks.shape)


def swapped(x, axis, offset=1):
    return lax.ppermute(x, axis, [(k, k ^ offset) for k in range(lax.axis_size(axis))])


def after(x, first):
    return lax.optimization_barrier((x, first))[0]


def shape(dims, dtype):
    return jax.ShapeDtypeStruct(dims, dtype)


def place(axis):
    return lax.axis_index(axis).astype(jnp.int32).reshape(1)


def on_device(image_emb, text_emb, factor):
    own_rows, width = image_emb.shape
    inner, chips = lax.axis_size(INNER), lax.axis_size(CHIPS)
    bf16, f32 = jnp.bfloat16, jnp.float32
    image_rows, text_rows = own_rows * inner, own_rows * chips
    wide = width + EXTRA
    work = 2 * image_rows * text_rows * width
    far, fars = place(FAR), lax.axis_size(FAR)
    tile = shape((8, 128), f32)

    text_copies = kernel_call(text_units_kernel, shape((text_rows, width), bf16), text_emb)
    text_own = exchanged(text_copies, CHIPS)
    text_other = swapped(text_own, CORE)
    half, diagonal = kernel_call(
        image_units_kernel, (shape((own_rows, width), bf16), tile), image_emb, text_emb
    )
    image_copies = kernel_call(
        join_kernel, shape((image_rows, width), bf16),
        far, half, *(swapped(half, FAR, k) for k in range(1, fars)),
    )
    image_group = exchanged(after(image_copies, text_own), NEAR)

    tile_of = (factor, image_group, text_own, text_other)
    row_message = kernel_call(
        rows_kernel, shape((inner, 8, 128), f32), *tile_of, diagonal, flops=2 * work
    )
    row_pieces = exchanged(row_message, INNER)
    col_part = kernel_call(columns_kernel, tile, *tile_of, flops=2 * work)
    col_message = kernel_call(
        pair_columns_kernel, shape((chips, 8, 128), f32), col_part, swapped(col_part, CORE)
    )
    col_pieces = exchanged(after(col_message, row_pieces), CHIPS)

    half_tile = shape((image_rows, text_rows), bf16)
    image_part, *weights, row_share = kernel_call(
        weights_kernel,
        (shape((image_rows, wide), bf16), half_tile, half_tile, tile),
        *tile_of, row_pieces, col_pieces,
        flops=4 * work,
    )
    own_part, other_part = kernel_call(
        text_sums_kernel,
        (shape((text_rows, width), f32), shape((text_rows, wide), bf16)),
        image_group, *weights, row_share,
        flops=2 * work,
    )
    image_pieces = exchanged(image_part, NEAR)
    text_part = kernel_call(
        pair_sums_kernel, shape((text_rows, wide), bf16),
        own_part, swapped(other_part, CORE), row_share,
    )
    text_pieces = exchanged(after(text_part, image_pieces), CHIPS)

    sent = [shape((own_rows, wide), bf16)] * (fars - 1)
    kept, *sent, share = kernel_call(
        near_sums_kernel, (shape((own_rows, width), f32), *sent, tile), far, image_pieces
    )
    out = shape((own_rows, width), f32)
    image_grad, share = kernel_call(
        image_gradient_kernel, (out, tile),
        factor, image_emb, text_emb, kept, share,
        *(swapped(block, FAR, k + 1) for k, block in enumerate(sent)),
    )
    whole = 2.0 * own_rows * inner * chips * lax.axis_size(CORE)
    text_grad, mean_loss = kernel_call(
        functools.partial(text_gradient_kernel, whole), (out, shape((1,), f32)),
        factor, text_emb, image_emb, text_pieces, share,
    )
    return (mean_loss, image_grad, text_grad)


def solution(mesh):
    split = Mesh(mesh.devices.reshape(2, 2, 2, 2, 4, 2, 2, 2), ALL)
    in_specs = (P(ALL, None), P(ALL, None), P())
    out_specs = (P(), P(ALL, None), P(ALL, None))
    return jax.shard_map(
        on_device, mesh=split, in_specs=in_specs, out_specs=out_specs, check_vma=False
    )
```

```python
import functools

import jax
import jax.numpy as jnp
from jax import lax
from jax.experimental import pallas as pl
from jax.experimental.pallas import tpu as pltpu
from jax.sharding import Mesh
from jax.sharding import PartitionSpec as P

ALL = ("z0", "y2", "y1", "y0", "x", "zh", "c")
INNER = ("z0", "y2", "y1", "y0")
CHIPS = ("x", "zh")
NEAR = ("z0", "y0")
FAR = ("y2", "y1")
CORE = "c"

EPSILON = 1e-06
LAST = (((1,), (1,)), ((), ()))
FIRST = (((0,), (0,)), ((), ()))
VMEM_LIMIT = 24 * 1024 * 1024
EXTRA = 128
LOG2_E = 1.4426950408889634


def f32_dot(a, b, dims):
    return lax.dot_general(a, b, dims, preferred_element_type=jnp.float32)


def unit_rows(values):
    inverse = lax.rsqrt(jnp.sum(values * values, axis=1, keepdims=True) + EPSILON)
    return values * inverse, inverse


def kernel_call(body, out_shape, *args, flops=0):
    def spec(a):
        return pl.BlockSpec(memory_space=pltpu.SMEM if a.size == 1 else pltpu.VMEM)

    outs = jax.tree.leaves(out_shape)
    moved = sum(a.size * a.dtype.itemsize for a in (*args, *outs))
    return pl.pallas_call(
        body,
        out_shape=out_shape,
        in_specs=[spec(a) for a in args],
        out_specs=jax.tree.map(spec, out_shape),
        compiler_params=pltpu.CompilerParams(vmem_limit_bytes=VMEM_LIMIT),
        cost_estimate=pl.CostEstimate(flops=flops, bytes_accessed=moved, transcendentals=0),
    )(*args)


def packed(value, rows):
    value = jnp.broadcast_to(value, (rows, EXTRA))
    high = value.astype(jnp.bfloat16).astype(jnp.float32)
    middle = (value - high).astype(jnp.bfloat16).astype(jnp.float32)
    low = value - high - middle
    lane = lax.broadcasted_iota(jnp.int32, (rows, EXTRA), 1)
    parts = jnp.where(lane == 0, high, jnp.where(lane == 1, middle, jnp.where(lane == 2, low, 0.0)))
    return parts.astype(jnp.bfloat16)


def unpacked(values, width):
    return jnp.sum(values[0:1, width:])


def text_units_kernel(values_ref, copies_ref):
    unit, _ = unit_rows(values_ref[...])
    half = jnp.concatenate([unit, unit], axis=0).astype(jnp.bfloat16)
    rows = half.shape[0]
    for k in range(copies_ref.shape[0] // rows):
        copies_ref[k * rows : (k + 1) * rows, :] = half


def image_units_kernel(values_ref, other_ref, half_ref, diagonal_ref):
    first = unit_rows(values_ref[...])[0].astype(jnp.bfloat16)
    second = unit_rows(other_ref[...])[0].astype(jnp.bfloat16)
    half_ref[...] = first
    products = first.astype(jnp.float32) * second.astype(jnp.float32)
    diagonal_ref[...] = jnp.broadcast_to(jnp.sum(products), diagonal_ref.shape)


def join_kernel(side_ref, mine_ref, theirs_ref, joined_ref):
    mine, theirs = mine_ref[...].astype(jnp.float32), theirs_ref[...].astype(jnp.float32)
    first = side_ref[0] == 0
    joined = jnp.concatenate(
        [jnp.where(first, mine, theirs), jnp.where(first, theirs, mine)], axis=0
    ).astype(jnp.bfloat16)
    rows = joined.shape[0]
    for k in range(joined_ref.shape[0] // rows):
        joined_ref[k * rows : (k + 1) * rows, :] = joined


def lines(row):
    return [row[:, k * 128 : (k + 1) * 128] for k in range(row.shape[1] // 128)]


def line(rows):
    return jnp.concatenate([rows[k : k + 1, :] for k in range(rows.shape[0])], axis=1)


def eight(rows):
    zero = jnp.zeros((1, 128), jnp.float32)
    return jnp.concatenate([*rows, *[zero] * (8 - len(rows))], axis=0)


def lse_of(parts):
    peak = functools.reduce(jnp.maximum, [jnp.max(p, axis=0, keepdims=True) for p in parts])
    total = sum(jnp.sum(jnp.exp2(p - peak), axis=0, keepdims=True) for p in parts)
    return peak + jnp.log2(total)


def pieces_lse(pieces):
    peak = jnp.max(pieces, axis=0)
    return peak + jnp.log2(jnp.sum(jnp.exp2(pieces - peak[None]), axis=0))


def pair_lse(a, b):
    peak = jnp.maximum(a, b)
    return peak + jnp.log2(jnp.exp2(a - peak) + jnp.exp2(b - peak))


def rows_kernel(factor_ref, image_ref, own_ref, other_ref, diagonal_ref, message_ref):
    factor = factor_ref[0] * LOG2_E
    image = image_ref[...]
    lse = lse_of([factor * f32_dot(text[...], image, LAST) for text in (own_ref, other_ref)])
    message = eight([*lines(lse), factor * diagonal_ref[0:1, :]])
    message_ref[...] = jnp.broadcast_to(message[None], message_ref.shape)


def columns_kernel(factor_ref, image_ref, own_ref, other_ref, message_ref):
    factor = factor_ref[0] * LOG2_E
    image = image_ref[...]
    own, other = (
        lse_of([factor * f32_dot(image, text[...], LAST)]) for text in (own_ref, other_ref)
    )
    message_ref[...] = eight([*lines(own), *lines(other)])


def pair_columns_kernel(mine_ref, theirs_ref, pair_ref):
    mine, theirs = mine_ref[...], theirs_ref[...]
    own = pair_lse(mine[0:3], theirs[3:6])
    other = pair_lse(mine[3:6], theirs[0:3])
    pair_ref[...] = jnp.concatenate([own, other, jnp.zeros((2, 128), jnp.float32)], axis=0)


def message_kernel(row_ref, pair_ref, message_ref):
    pieces = row_ref[...]
    share = jnp.sum(pieces_lse(pieces)[0:3]) - 2.0 * jnp.max(jnp.sum(pieces, axis=0)[3:4])
    number = lax.broadcasted_iota(jnp.int32, (8, 128), 0)
    message = jnp.where(number == 6, share, pair_ref[...])
    message_ref[...] = jnp.broadcast_to(message[None], message_ref.shape)


def weights_kernel(
    factor_ref, image_ref, own_ref, other_ref, row_ref, pieces_ref,
    image_out, own_out, other_out, share_ref,
):
    factor = factor_ref[0]
    width = own_ref.shape[1]
    pieces = pieces_ref[...]
    cols = pieces_lse(pieces)
    own_lse, other_lse = line(cols[0:3]), line(cols[3:6])
    col_share = jnp.sum(own_lse) + jnp.sum(other_lse)
    rows = pieces_lse(row_ref[...])[0:3]
    row_share = jnp.max(jnp.sum(pieces, axis=0)[6:7])
    share_ref[...] = jnp.broadcast_to(row_share, share_ref.shape)
    row_lse = jnp.concatenate(
        [jnp.transpose(jnp.broadcast_to(rows[k : k + 1, :], (128, 128))) for k in range(3)], axis=0
    )[:, 0:1]
    image = image_ref[...]
    sums = []
    for text_ref, weights_ref, col_lse in (
        (own_ref, own_out, own_lse), (other_ref, other_out, other_lse)
    ):
        text = text_ref[...]
        logits = (factor * LOG2_E) * f32_dot(image, text, LAST)
        weights = (
            (0.5 * factor) * (jnp.exp2(logits - row_lse) + jnp.exp2(logits - col_lse))
        ).astype(jnp.bfloat16)
        weights_ref[...] = weights
        sums.append(jnp.dot(weights, text, preferred_element_type=jnp.float32))
    image_out[:, :width] = (sums[0] + sums[1]).astype(jnp.bfloat16)
    image_out[:, width:] = packed(col_share, image_out.shape[0])


def text_sums_kernel(image_ref, own_ref, other_ref, share_ref, own_out, other_out):
    image = image_ref[...]
    width = image.shape[1]
    other_out[:, :width] = f32_dot(other_ref[...], image, FIRST).astype(jnp.bfloat16)
    other_out[:, width:] = packed(jnp.max(share_ref[...]), other_out.shape[0])
    own_out[...] = f32_dot(own_ref[...], image, FIRST)


def pair_sums_kernel(own_ref, theirs_ref, shared_ref, sums_ref, share_ref):
    width = own_ref.shape[1]
    theirs = theirs_ref[...].astype(jnp.float32)
    sums_ref[...] = (own_ref[...] + theirs[:, :width]).astype(jnp.bfloat16)
    share = jnp.max(shared_ref[...]) + unpacked(theirs, width)
    share_ref[...] = jnp.broadcast_to(share, share_ref.shape)


def slabs_sum(pieces_ref, rows):
    total = None
    for k in range(pieces_ref.shape[0] // (2 * rows)):
        both = pieces_ref[2 * rows * k : 2 * rows * (k + 1), :].astype(jnp.float32)
        both = both[:rows] + both[rows:]
        total = both if total is None else total + both
    return total


def keep_and_send(total, share, side_ref, keep_ref, send_ref, share_ref):
    rows, width = keep_ref.shape
    first = side_ref[0] == 0
    lower, upper = total[:rows, :width], total[rows:, :width]
    keep_ref[...] = jnp.where(first, lower, upper)
    send_ref[:, :width] = jnp.where(first, upper, lower).astype(jnp.bfloat16)
    send_ref[:, width:] = packed(share, rows)
    share_ref[...] = jnp.broadcast_to(share, share_ref.shape)


def near_sums_kernel(side_ref, pieces_ref, keep_ref, send_ref, share_ref):
    rows, width = keep_ref.shape
    total = slabs_sum(pieces_ref, 2 * rows)
    keep_and_send(total, unpacked(total, width), side_ref, keep_ref, send_ref, share_ref)


def middle_sums_kernel(side_ref, kept_ref, theirs_ref, shared_ref, keep_ref, send_ref, share_ref):
    width = kept_ref.shape[1]
    theirs = theirs_ref[...].astype(jnp.float32)
    share = jnp.max(shared_ref[...]) + unpacked(theirs, width)
    keep_and_send(kept_ref[...] + theirs[:, :width], share, side_ref, keep_ref, send_ref, share_ref)


def gradient(factor, values, paired, total):
    unit, inverse = unit_rows(values)
    pull = total - factor * unit_rows(paired)[0].astype(jnp.bfloat16).astype(jnp.float32)
    return (pull - unit * jnp.sum(pull * unit, axis=1, keepdims=True)) * inverse


def image_gradient_kernel(
    factor_ref, values_ref, paired_ref, kept_ref, theirs_ref, shared_ref, gradient_ref, share_ref
):
    width = kept_ref.shape[1]
    theirs = theirs_ref[...].astype(jnp.float32)
    total = kept_ref[...] + theirs[:, :width]
    gradient_ref[...] = gradient(factor_ref[0], values_ref[...], paired_ref[...], total)
    share = jnp.max(shared_ref[...]) + unpacked(theirs, width)
    share_ref[...] = jnp.broadcast_to(share, share_ref.shape)


def text_gradient_kernel(
    whole, factor_ref, values_ref, paired_ref, pieces_ref, row_share_ref, col_share_ref,
    gradient_ref, loss_ref,
):
    total = slabs_sum(pieces_ref, values_ref.shape[0])
    gradient_ref[...] = gradient(factor_ref[0], values_ref[...], paired_ref[...], total)
    loss_ref[0] = jnp.max(row_share_ref[...] + col_share_ref[...]) * (1.0 / (LOG2_E * whole))


def exchanged(blocks, axis):
    count = lax.axis_size(axis)
    split = blocks.reshape(count, -1, blocks.shape[-1])
    return lax.all_to_all(split, axis, split_axis=0, concat_axis=0, tiled=True).reshape(blocks.shape)


def swapped(x, axis, offset=1):
    return lax.ppermute(x, axis, [(k, k ^ offset) for k in range(lax.axis_size(axis))])


def after(x, first):
    return lax.optimization_barrier((x, first))[0]


def shape(dims, dtype):
    return jax.ShapeDtypeStruct(dims, dtype)


def place(axis):
    return lax.axis_index(axis).astype(jnp.int32).reshape(1)


def on_device(image_emb, text_emb, factor):
    own_rows, width = image_emb.shape
    inner, chips = lax.axis_size(INNER), lax.axis_size(CHIPS)
    bf16, f32 = jnp.bfloat16, jnp.float32
    image_rows, text_rows = own_rows * inner, own_rows * chips
    wide = width + EXTRA
    work = 2 * image_rows * text_rows * width
    high, low = place(FAR[0]), place(FAR[1])
    tile = shape((8, 128), f32)

    text_copies = kernel_call(text_units_kernel, shape((text_rows, width), bf16), text_emb)
    text_own = exchanged(text_copies, CHIPS)
    text_other = swapped(text_own, CORE)
    half, diagonal = kernel_call(
        image_units_kernel, (shape((own_rows, width), bf16), tile), image_emb, text_emb
    )
    two = kernel_call(
        join_kernel, shape((2 * own_rows, width), bf16), low, half, swapped(half, FAR, 1)
    )
    image_copies = kernel_call(
        join_kernel, shape((image_rows, width), bf16), high, two, swapped(two, FAR, 3)
    )
    image_group = exchanged(after(image_copies, text_own), NEAR)

    tile_of = (factor, image_group, text_own, text_other)
    row_message = kernel_call(
        rows_kernel, shape((inner, 8, 128), f32), *tile_of, diagonal, flops=2 * work
    )
    row_pieces = exchanged(row_message, INNER)
    col_part = kernel_call(columns_kernel, tile, *tile_of, flops=2 * work)
    pair = kernel_call(pair_columns_kernel, tile, col_part, swapped(col_part, CORE))
    col_message = kernel_call(
        message_kernel, shape((chips, 8, 128), f32), row_pieces, pair
    )
    col_pieces = exchanged(col_message, CHIPS)

    half_tile = shape((image_rows, text_rows), bf16)
    image_part, *weights, row_share = kernel_call(
        weights_kernel,
        (shape((image_rows, wide), bf16), half_tile, half_tile, tile),
        *tile_of, row_pieces, col_pieces,
        flops=4 * work,
    )
    own_part, other_part = kernel_call(
        text_sums_kernel,
        (shape((text_rows, width), f32), shape((text_rows, wide), bf16)),
        image_group, *weights, row_share,
        flops=2 * work,
    )
    image_pieces = exchanged(image_part, NEAR)
    text_part, row_share = kernel_call(
        pair_sums_kernel, (shape((text_rows, width), bf16), tile),
        own_part, swapped(other_part, CORE), row_share,
    )
    text_pieces = exchanged(after(text_part, image_pieces), CHIPS)

    kept, sent, share = kernel_call(
        near_sums_kernel,
        (shape((2 * own_rows, width), f32), shape((2 * own_rows, wide), bf16), tile),
        high, image_pieces,
    )
    kept, sent, share = kernel_call(
        middle_sums_kernel,
        (shape((own_rows, width), f32), shape((own_rows, wide), bf16), tile),
        low, kept, swapped(sent, FAR, 3), share,
    )
    out = shape((own_rows, width), f32)
    image_grad, share = kernel_call(
        image_gradient_kernel, (out, tile),
        factor, image_emb, text_emb, kept, swapped(sent, FAR, 1), share,
    )
    whole = 2.0 * own_rows * inner * chips * lax.axis_size(CORE)
    text_grad, mean_loss = kernel_call(
        functools.partial(text_gradient_kernel, whole), (out, shape((1,), f32)),
        factor, text_emb, image_emb, text_pieces, row_share, share,
    )
    return (mean_loss, image_grad, text_grad)


def solution(mesh):
    split = Mesh(mesh.devices.reshape(2, 2, 2, 2, 4, 4, 2), ALL)
    in_specs = (P(ALL, None), P(ALL, None), P())
    out_specs = (P(), P(ALL, None), P(ALL, None))
    return jax.shard_map(
        on_device, mesh=split, in_specs=in_specs, out_specs=out_specs, check_vma=False
    )
```

```python
import functools

import jax
import jax.numpy as jnp
from jax import lax
from jax.experimental import pallas as pl
from jax.experimental.pallas import tpu as pltpu
from jax.sharding import Mesh
from jax.sharding import PartitionSpec as P

ALL = ("z0", "y2", "y1", "y0", "x", "zh", "c")
INNER = ("y2", "y1", "x")
CHIPS = ("y0", "zh", "z0")
NEAR = "x"
FAR = ("y2", "y1")
CORE = "c"

EPSILON = 1e-06
LAST = (((1,), (1,)), ((), ()))
FIRST = (((0,), (0,)), ((), ()))
VMEM_LIMIT = 24 * 1024 * 1024
EXTRA = 128
LOG2_E = 1.4426950408889634


def f32_dot(a, b, dims):
    return lax.dot_general(a, b, dims, preferred_element_type=jnp.float32)


def unit_rows(values):
    inverse = lax.rsqrt(jnp.sum(values * values, axis=1, keepdims=True) + EPSILON)
    return values * inverse, inverse


def kernel_call(body, out_shape, *args, flops=0):
    def spec(a):
        return pl.BlockSpec(memory_space=pltpu.SMEM if a.size == 1 else pltpu.VMEM)

    outs = jax.tree.leaves(out_shape)
    moved = sum(a.size * a.dtype.itemsize for a in (*args, *outs))
    return pl.pallas_call(
        body,
        out_shape=out_shape,
        in_specs=[spec(a) for a in args],
        out_specs=jax.tree.map(spec, out_shape),
        compiler_params=pltpu.CompilerParams(vmem_limit_bytes=VMEM_LIMIT),
        cost_estimate=pl.CostEstimate(flops=flops, bytes_accessed=moved, transcendentals=0),
    )(*args)


def packed(value, rows):
    value = jnp.broadcast_to(value, (rows, EXTRA))
    high = value.astype(jnp.bfloat16).astype(jnp.float32)
    middle = (value - high).astype(jnp.bfloat16).astype(jnp.float32)
    low = value - high - middle
    lane = lax.broadcasted_iota(jnp.int32, (rows, EXTRA), 1)
    parts = jnp.where(lane == 0, high, jnp.where(lane == 1, middle, jnp.where(lane == 2, low, 0.0)))
    return parts.astype(jnp.bfloat16)


def unpacked(values, width):
    return jnp.sum(values[0:1, width:])


def text_units_kernel(values_ref, copies_ref):
    unit, _ = unit_rows(values_ref[...])
    half = jnp.concatenate([unit, unit], axis=0).astype(jnp.bfloat16)
    rows = half.shape[0]
    for k in range(copies_ref.shape[0] // rows):
        copies_ref[k * rows : (k + 1) * rows, :] = half


def image_units_kernel(values_ref, other_ref, half_ref, diagonal_ref):
    first = unit_rows(values_ref[...])[0].astype(jnp.bfloat16)
    second = unit_rows(other_ref[...])[0].astype(jnp.bfloat16)
    half_ref[...] = first
    products = first.astype(jnp.float32) * second.astype(jnp.float32)
    diagonal_ref[...] = jnp.broadcast_to(jnp.sum(products), diagonal_ref.shape)


def join_kernel(side_ref, mine_ref, theirs_ref, joined_ref):
    mine, theirs = mine_ref[...].astype(jnp.float32), theirs_ref[...].astype(jnp.float32)
    first = side_ref[0] == 0
    joined = jnp.concatenate(
        [jnp.where(first, mine, theirs), jnp.where(first, theirs, mine)], axis=0
    ).astype(jnp.bfloat16)
    rows = joined.shape[0]
    for k in range(joined_ref.shape[0] // rows):
        joined_ref[k * rows : (k + 1) * rows, :] = joined


def lines(row):
    return [row[:, k * 128 : (k + 1) * 128] for k in range(row.shape[1] // 128)]


def line(rows):
    return jnp.concatenate([rows[k : k + 1, :] for k in range(rows.shape[0])], axis=1)


def eight(rows):
    zero = jnp.zeros((1, 128), jnp.float32)
    return jnp.concatenate([*rows, *[zero] * (8 - len(rows))], axis=0)


def lse_of(parts):
    peak = functools.reduce(jnp.maximum, [jnp.max(p, axis=0, keepdims=True) for p in parts])
    total = sum(jnp.sum(jnp.exp2(p - peak), axis=0, keepdims=True) for p in parts)
    return peak + jnp.log2(total)


def pieces_lse(pieces):
    peak = jnp.max(pieces, axis=0)
    return peak + jnp.log2(jnp.sum(jnp.exp2(pieces - peak[None]), axis=0))


def pair_lse(a, b):
    peak = jnp.maximum(a, b)
    return peak + jnp.log2(jnp.exp2(a - peak) + jnp.exp2(b - peak))


def rows_kernel(factor_ref, image_ref, own_ref, other_ref, diagonal_ref, message_ref):
    factor = factor_ref[0] * LOG2_E
    image = image_ref[...]
    lse = lse_of([factor * f32_dot(text[...], image, LAST) for text in (own_ref, other_ref)])
    message = eight([*lines(lse), factor * diagonal_ref[0:1, :]])
    message_ref[...] = jnp.broadcast_to(message[None], message_ref.shape)


def columns_kernel(factor_ref, image_ref, own_ref, other_ref, message_ref):
    factor = factor_ref[0] * LOG2_E
    image = image_ref[...]
    own, other = (
        lse_of([factor * f32_dot(image, text[...], LAST)]) for text in (own_ref, other_ref)
    )
    message_ref[...] = eight([*lines(own), *lines(other)])


def pair_columns_kernel(core_ref, both_ref, pair_ref):
    mine, theirs = both_ref[core_ref[0]], both_ref[1 - core_ref[0]]
    own = pair_lse(mine[0:3], theirs[3:6])
    other = pair_lse(mine[3:6], theirs[0:3])
    pair_ref[...] = jnp.concatenate([own, other, jnp.zeros((2, 128), jnp.float32)], axis=0)


def message_kernel(row_ref, pair_ref, message_ref):
    pieces = row_ref[...]
    share = jnp.sum(pieces_lse(pieces)[0:3]) - 2.0 * jnp.max(jnp.sum(pieces, axis=0)[3:4])
    number = lax.broadcasted_iota(jnp.int32, (8, 128), 0)
    message = jnp.where(number == 6, share, pair_ref[...])
    message_ref[...] = jnp.broadcast_to(message[None], message_ref.shape)


def weights_kernel(
    factor_ref, image_ref, own_ref, other_ref, row_ref, pieces_ref,
    image_out, own_out, other_out, share_ref,
):
    factor = factor_ref[0]
    width = own_ref.shape[1]
    pieces = pieces_ref[...]
    cols = pieces_lse(pieces)
    own_lse, other_lse = line(cols[0:3]), line(cols[3:6])
    col_share = jnp.sum(own_lse) + jnp.sum(other_lse)
    rows = pieces_lse(row_ref[...])[0:3]
    row_share = jnp.max(jnp.sum(pieces, axis=0)[6:7])
    share_ref[...] = jnp.broadcast_to(row_share, share_ref.shape)
    row_lse = jnp.concatenate(
        [jnp.transpose(jnp.broadcast_to(rows[k : k + 1, :], (128, 128))) for k in range(3)], axis=0
    )[:, 0:1]
    image = image_ref[...]
    sums = []
    for text_ref, weights_ref, col_lse in (
        (own_ref, own_out, own_lse), (other_ref, other_out, other_lse)
    ):
        text = text_ref[...]
        logits = (factor * LOG2_E) * f32_dot(image, text, LAST)
        weights = (
            (0.5 * factor) * (jnp.exp2(logits - row_lse) + jnp.exp2(logits - col_lse))
        ).astype(jnp.bfloat16)
        weights_ref[...] = weights
        sums.append(jnp.dot(weights, text, preferred_element_type=jnp.float32))
    image_out[:, :width] = (sums[0] + sums[1]).astype(jnp.bfloat16)
    image_out[:, width:] = packed(col_share, image_out.shape[0])


def text_sums_kernel(image_ref, own_ref, other_ref, share_ref, own_out, other_out):
    image = image_ref[...]
    width = image.shape[1]
    other_out[:, :width] = f32_dot(other_ref[...], image, FIRST).astype(jnp.bfloat16)
    other_out[:, width:] = packed(jnp.max(share_ref[...]), other_out.shape[0])
    own_out[...] = f32_dot(own_ref[...], image, FIRST)


def pair_sums_kernel(own_ref, theirs_ref, shared_ref, sums_ref, share_ref):
    width = own_ref.shape[1]
    theirs = theirs_ref[...].astype(jnp.float32)
    sums_ref[...] = (own_ref[...] + theirs[:, :width]).astype(jnp.bfloat16)
    share = jnp.max(shared_ref[...]) + unpacked(theirs, width)
    share_ref[...] = jnp.broadcast_to(share, share_ref.shape)


def slabs_sum(pieces_ref, rows):
    total = None
    for k in range(pieces_ref.shape[0] // (2 * rows)):
        both = pieces_ref[2 * rows * k : 2 * rows * (k + 1), :].astype(jnp.float32)
        both = both[:rows] + both[rows:]
        total = both if total is None else total + both
    return total


def keep_and_send(total, share, side_ref, keep_ref, send_ref, share_ref):
    rows, width = keep_ref.shape
    first = side_ref[0] == 0
    lower, upper = total[:rows, :width], total[rows:, :width]
    keep_ref[...] = jnp.where(first, lower, upper)
    send_ref[:, :width] = jnp.where(first, upper, lower).astype(jnp.bfloat16)
    send_ref[:, width:] = packed(share, rows)
    share_ref[...] = jnp.broadcast_to(share, share_ref.shape)


def near_sums_kernel(side_ref, pieces_ref, keep_ref, send_ref, share_ref):
    rows, width = keep_ref.shape
    total = slabs_sum(pieces_ref, 2 * rows)
    keep_and_send(total, unpacked(total, width), side_ref, keep_ref, send_ref, share_ref)


def middle_sums_kernel(side_ref, kept_ref, theirs_ref, shared_ref, keep_ref, send_ref, share_ref):
    width = kept_ref.shape[1]
    theirs = theirs_ref[...].astype(jnp.float32)
    share = jnp.max(shared_ref[...]) + unpacked(theirs, width)
    keep_and_send(kept_ref[...] + theirs[:, :width], share, side_ref, keep_ref, send_ref, share_ref)


def gradient(factor, values, paired, total):
    unit, inverse = unit_rows(values)
    pull = total - factor * unit_rows(paired)[0].astype(jnp.bfloat16).astype(jnp.float32)
    return (pull - unit * jnp.sum(pull * unit, axis=1, keepdims=True)) * inverse


def image_gradient_kernel(
    factor_ref, values_ref, paired_ref, kept_ref, theirs_ref, shared_ref, gradient_ref, share_ref
):
    width = kept_ref.shape[1]
    theirs = theirs_ref[...].astype(jnp.float32)
    total = kept_ref[...] + theirs[:, :width]
    gradient_ref[...] = gradient(factor_ref[0], values_ref[...], paired_ref[...], total)
    share = jnp.max(shared_ref[...]) + unpacked(theirs, width)
    share_ref[...] = jnp.broadcast_to(share, share_ref.shape)


def text_gradient_kernel(
    whole, factor_ref, values_ref, paired_ref, pieces_ref, row_share_ref, col_share_ref,
    gradient_ref, loss_ref,
):
    total = slabs_sum(pieces_ref, values_ref.shape[0])
    gradient_ref[...] = gradient(factor_ref[0], values_ref[...], paired_ref[...], total)
    loss_ref[0] = jnp.max(row_share_ref[...] + col_share_ref[...]) * (1.0 / (LOG2_E * whole))


def exchanged(blocks, axis):
    count = lax.axis_size(axis)
    split = blocks.reshape(count, -1, blocks.shape[-1])
    return lax.all_to_all(split, axis, split_axis=0, concat_axis=0, tiled=True).reshape(blocks.shape)


def swapped(x, axis, offset=1):
    return lax.ppermute(x, axis, [(k, k ^ offset) for k in range(lax.axis_size(axis))])


def after(x, first):
    return lax.optimization_barrier((x, first))[0]


def shape(dims, dtype):
    return jax.ShapeDtypeStruct(dims, dtype)


def place(axis):
    return lax.axis_index(axis).astype(jnp.int32).reshape(1)


def on_device(image_emb, text_emb, factor):
    own_rows, width = image_emb.shape
    inner, chips = lax.axis_size(INNER), lax.axis_size(CHIPS)
    bf16, f32 = jnp.bfloat16, jnp.float32
    image_rows, text_rows = own_rows * inner, own_rows * chips
    wide = width + EXTRA
    work = 2 * image_rows * text_rows * width
    high, low, core = place(FAR[0]), place(FAR[1]), place(CORE)
    tile = shape((8, 128), f32)

    text_copies = kernel_call(text_units_kernel, shape((text_rows, width), bf16), text_emb)
    text_own = exchanged(text_copies, CHIPS)
    text_other = swapped(text_own, CORE)
    half, diagonal = kernel_call(
        image_units_kernel, (shape((own_rows, width), bf16), tile), image_emb, text_emb
    )
    two = kernel_call(
        join_kernel, shape((2 * own_rows, width), bf16), low, half, swapped(half, FAR, 1)
    )
    image_copies = kernel_call(
        join_kernel, shape((image_rows, width), bf16), high, two, swapped(two, FAR, 3)
    )
    image_group = exchanged(after(image_copies, text_own), NEAR)

    tile_of = (factor, image_group, text_own, text_other)
    row_message = kernel_call(
        rows_kernel, shape((inner, 8, 128), f32), *tile_of, diagonal, flops=2 * work
    )
    row_pieces = exchanged(row_message, INNER)
    col_part = kernel_call(columns_kernel, tile, *tile_of, flops=2 * work)
    pair = kernel_call(pair_columns_kernel, tile, core, lax.all_gather(col_part, CORE))
    col_message = kernel_call(
        message_kernel, shape((chips, 8, 128), f32), row_pieces, pair
    )
    col_pieces = exchanged(col_message, CHIPS)

    half_tile = shape((image_rows, text_rows), bf16)
    image_part, *weights, row_share = kernel_call(
        weights_kernel,
        (shape((image_rows, wide), bf16), half_tile, half_tile, tile),
        *tile_of, row_pieces, col_pieces,
        flops=4 * work,
    )
    own_part, other_part = kernel_call(
        text_sums_kernel,
        (shape((text_rows, width), f32), shape((text_rows, wide), bf16)),
        image_group, *weights, row_share,
        flops=2 * work,
    )
    image_pieces = exchanged(image_part, NEAR)
    text_part, row_share = kernel_call(
        pair_sums_kernel, (shape((text_rows, width), bf16), tile),
        own_part, swapped(other_part, CORE), row_share,
    )
    text_pieces = exchanged(after(text_part, image_pieces), CHIPS)

    kept, sent, share = kernel_call(
        near_sums_kernel,
        (shape((2 * own_rows, width), f32), shape((2 * own_rows, wide), bf16), tile),
        high, image_pieces,
    )
    kept, sent, share = kernel_call(
        middle_sums_kernel,
        (shape((own_rows, width), f32), shape((own_rows, wide), bf16), tile),
        low, kept, swapped(sent, FAR, 3), share,
    )
    out = shape((own_rows, width), f32)
    image_grad, share = kernel_call(
        image_gradient_kernel, (out, tile),
        factor, image_emb, text_emb, kept, swapped(sent, FAR, 1), share,
    )
    whole = 2.0 * own_rows * inner * chips * lax.axis_size(CORE)
    text_grad, mean_loss = kernel_call(
        functools.partial(text_gradient_kernel, whole), (out, shape((1,), f32)),
        factor, text_emb, image_emb, text_pieces, row_share, share,
    )
    return (mean_loss, image_grad, text_grad)


def solution(mesh):
    split = Mesh(mesh.devices.reshape(2, 2, 2, 2, 4, 4, 2), ALL)
    in_specs = (P(ALL, None), P(ALL, None), P())
    out_specs = (P(), P(ALL, None), P(ALL, None))
    return jax.shard_map(
        on_device, mesh=split, in_specs=in_specs, out_specs=out_specs, check_vma=False
    )
```

```python
import functools

import jax
import jax.numpy as jnp
from jax import lax
from jax.experimental import pallas as pl
from jax.experimental.pallas import tpu as pltpu
from jax.sharding import Mesh
from jax.sharding import PartitionSpec as P

ALL = ("z0", "y2", "y1", "y0", "x", "z2", "z1", "c")
INNER = ("z2", "z1", "z0", "y0")
CHIPS = ("x", "y2", "y1")
NEAR = ("z0", "y0")
FAR = ("z2", "z1")
CORE = "c"

EPSILON = 1e-06
LAST = (((1,), (1,)), ((), ()))
FIRST = (((0,), (0,)), ((), ()))
VMEM_LIMIT = 24 * 1024 * 1024
EXTRA = 128
LOG2_E = 1.4426950408889634


def f32_dot(a, b, dims):
    return lax.dot_general(a, b, dims, preferred_element_type=jnp.float32)


def unit_rows(values):
    inverse = lax.rsqrt(jnp.sum(values * values, axis=1, keepdims=True) + EPSILON)
    return values * inverse, inverse


def kernel_call(body, out_shape, *args, flops=0):
    def spec(a):
        return pl.BlockSpec(memory_space=pltpu.SMEM if a.size == 1 else pltpu.VMEM)

    outs = jax.tree.leaves(out_shape)
    moved = sum(a.size * a.dtype.itemsize for a in (*args, *outs))
    return pl.pallas_call(
        body,
        out_shape=out_shape,
        in_specs=[spec(a) for a in args],
        out_specs=jax.tree.map(spec, out_shape),
        compiler_params=pltpu.CompilerParams(vmem_limit_bytes=VMEM_LIMIT),
        cost_estimate=pl.CostEstimate(flops=flops, bytes_accessed=moved, transcendentals=0),
    )(*args)


def packed(value, rows):
    value = jnp.broadcast_to(value, (rows, EXTRA))
    high = value.astype(jnp.bfloat16).astype(jnp.float32)
    middle = (value - high).astype(jnp.bfloat16).astype(jnp.float32)
    low = value - high - middle
    lane = lax.broadcasted_iota(jnp.int32, (rows, EXTRA), 1)
    parts = jnp.where(lane == 0, high, jnp.where(lane == 1, middle, jnp.where(lane == 2, low, 0.0)))
    return parts.astype(jnp.bfloat16)


def unpacked(values, width):
    return jnp.sum(values[0:1, width:])


def text_units_kernel(values_ref, copies_ref):
    unit, _ = unit_rows(values_ref[...])
    half = jnp.concatenate([unit, unit], axis=0).astype(jnp.bfloat16)
    rows = half.shape[0]
    for k in range(copies_ref.shape[0] // rows):
        copies_ref[k * rows : (k + 1) * rows, :] = half


def image_units_kernel(values_ref, other_ref, half_ref, diagonal_ref):
    first = unit_rows(values_ref[...])[0].astype(jnp.bfloat16)
    second = unit_rows(other_ref[...])[0].astype(jnp.bfloat16)
    half_ref[...] = first
    products = first.astype(jnp.float32) * second.astype(jnp.float32)
    diagonal_ref[...] = jnp.broadcast_to(jnp.sum(products), diagonal_ref.shape)


def join_kernel(side_ref, mine_ref, theirs_ref, joined_ref):
    mine, theirs = mine_ref[...].astype(jnp.float32), theirs_ref[...].astype(jnp.float32)
    first = side_ref[0] == 0
    joined = jnp.concatenate(
        [jnp.where(first, mine, theirs), jnp.where(first, theirs, mine)], axis=0
    ).astype(jnp.bfloat16)
    rows = joined.shape[0]
    for k in range(joined_ref.shape[0] // rows):
        joined_ref[k * rows : (k + 1) * rows, :] = joined


def lines(row):
    return [row[:, k * 128 : (k + 1) * 128] for k in range(row.shape[1] // 128)]


def line(rows):
    return jnp.concatenate([rows[k : k + 1, :] for k in range(rows.shape[0])], axis=1)


def eight(rows):
    zero = jnp.zeros((1, 128), jnp.float32)
    return jnp.concatenate([*rows, *[zero] * (8 - len(rows))], axis=0)


def lse_of(parts):
    peak = functools.reduce(jnp.maximum, [jnp.max(p, axis=0, keepdims=True) for p in parts])
    total = sum(jnp.sum(jnp.exp2(p - peak), axis=0, keepdims=True) for p in parts)
    return peak + jnp.log2(total)


def pieces_lse(pieces):
    peak = jnp.max(pieces, axis=0)
    return peak + jnp.log2(jnp.sum(jnp.exp2(pieces - peak[None]), axis=0))


def pair_lse(a, b):
    peak = jnp.maximum(a, b)
    return peak + jnp.log2(jnp.exp2(a - peak) + jnp.exp2(b - peak))


def rows_kernel(factor_ref, image_ref, own_ref, other_ref, diagonal_ref, message_ref):
    factor = factor_ref[0] * LOG2_E
    image = image_ref[...]
    lse = lse_of([factor * f32_dot(text[...], image, LAST) for text in (own_ref, other_ref)])
    message = eight([*lines(lse), factor * diagonal_ref[0:1, :]])
    message_ref[...] = jnp.broadcast_to(message[None], message_ref.shape)


def columns_kernel(factor_ref, image_ref, own_ref, other_ref, message_ref):
    factor = factor_ref[0] * LOG2_E
    image = image_ref[...]
    own, other = (
        lse_of([factor * f32_dot(image, text[...], LAST)]) for text in (own_ref, other_ref)
    )
    message_ref[...] = eight([*lines(own), *lines(other)])


def pair_columns_kernel(mine_ref, theirs_ref, pair_ref):
    mine, theirs = mine_ref[...], theirs_ref[...]
    own = pair_lse(mine[0:3], theirs[3:6])
    other = pair_lse(mine[3:6], theirs[0:3])
    pair_ref[...] = jnp.concatenate([own, other, jnp.zeros((2, 128), jnp.float32)], axis=0)


def message_kernel(row_ref, pair_ref, message_ref):
    pieces = row_ref[...]
    share = jnp.sum(pieces_lse(pieces)[0:3]) - 2.0 * jnp.max(jnp.sum(pieces, axis=0)[3:4])
    number = lax.broadcasted_iota(jnp.int32, (8, 128), 0)
    message = jnp.where(number == 6, share, pair_ref[...])
    message_ref[...] = jnp.broadcast_to(message[None], message_ref.shape)


def weights_kernel(
    factor_ref, image_ref, own_ref, other_ref, row_ref, pieces_ref,
    image_out, own_out, other_out, share_ref,
):
    factor = factor_ref[0]
    width = own_ref.shape[1]
    pieces = pieces_ref[...]
    cols = pieces_lse(pieces)
    own_lse, other_lse = line(cols[0:3]), line(cols[3:6])
    col_share = jnp.sum(own_lse) + jnp.sum(other_lse)
    rows = pieces_lse(row_ref[...])[0:3]
    row_share = jnp.max(jnp.sum(pieces, axis=0)[6:7])
    share_ref[...] = jnp.broadcast_to(row_share, share_ref.shape)
    row_lse = jnp.concatenate(
        [jnp.transpose(jnp.broadcast_to(rows[k : k + 1, :], (128, 128))) for k in range(3)], axis=0
    )[:, 0:1]
    image = image_ref[...]
    sums = []
    for text_ref, weights_ref, col_lse in (
        (own_ref, own_out, own_lse), (other_ref, other_out, other_lse)
    ):
        text = text_ref[...]
        logits = (factor * LOG2_E) * f32_dot(image, text, LAST)
        weights = (
            (0.5 * factor) * (jnp.exp2(logits - row_lse) + jnp.exp2(logits - col_lse))
        ).astype(jnp.bfloat16)
        weights_ref[...] = weights
        sums.append(jnp.dot(weights, text, preferred_element_type=jnp.float32))
    image_out[:, :width] = (sums[0] + sums[1]).astype(jnp.bfloat16)
    image_out[:, width:] = packed(col_share, image_out.shape[0])


def text_sums_kernel(image_ref, own_ref, other_ref, share_ref, own_out, other_out):
    image = image_ref[...]
    width = image.shape[1]
    other_out[:, :width] = f32_dot(other_ref[...], image, FIRST).astype(jnp.bfloat16)
    other_out[:, width:] = packed(jnp.max(share_ref[...]), other_out.shape[0])
    own_out[...] = f32_dot(own_ref[...], image, FIRST)


def pair_sums_kernel(own_ref, theirs_ref, shared_ref, sums_ref, share_ref):
    width = own_ref.shape[1]
    theirs = theirs_ref[...].astype(jnp.float32)
    sums_ref[...] = (own_ref[...] + theirs[:, :width]).astype(jnp.bfloat16)
    share = jnp.max(shared_ref[...]) + unpacked(theirs, width)
    share_ref[...] = jnp.broadcast_to(share, share_ref.shape)


def slabs_sum(pieces_ref, rows):
    total = None
    for k in range(pieces_ref.shape[0] // (2 * rows)):
        both = pieces_ref[2 * rows * k : 2 * rows * (k + 1), :].astype(jnp.float32)
        both = both[:rows] + both[rows:]
        total = both if total is None else total + both
    return total


def keep_and_send(total, share, side_ref, keep_ref, send_ref, share_ref):
    rows, width = keep_ref.shape
    first = side_ref[0] == 0
    lower, upper = total[:rows, :width], total[rows:, :width]
    keep_ref[...] = jnp.where(first, lower, upper)
    send_ref[:, :width] = jnp.where(first, upper, lower).astype(jnp.bfloat16)
    send_ref[:, width:] = packed(share, rows)
    share_ref[...] = jnp.broadcast_to(share, share_ref.shape)


def near_sums_kernel(side_ref, pieces_ref, keep_ref, send_ref, share_ref):
    rows, width = keep_ref.shape
    total = slabs_sum(pieces_ref, 2 * rows)
    keep_and_send(total, unpacked(total, width), side_ref, keep_ref, send_ref, share_ref)


def middle_sums_kernel(side_ref, kept_ref, theirs_ref, shared_ref, keep_ref, send_ref, share_ref):
    width = kept_ref.shape[1]
    theirs = theirs_ref[...].astype(jnp.float32)
    share = jnp.max(shared_ref[...]) + unpacked(theirs, width)
    keep_and_send(kept_ref[...] + theirs[:, :width], share, side_ref, keep_ref, send_ref, share_ref)


def gradient(factor, values, paired, total):
    unit, inverse = unit_rows(values)
    pull = total - factor * unit_rows(paired)[0].astype(jnp.bfloat16).astype(jnp.float32)
    return (pull - unit * jnp.sum(pull * unit, axis=1, keepdims=True)) * inverse


def image_gradient_kernel(
    factor_ref, values_ref, paired_ref, kept_ref, theirs_ref, shared_ref, gradient_ref, share_ref
):
    width = kept_ref.shape[1]
    theirs = theirs_ref[...].astype(jnp.float32)
    total = kept_ref[...] + theirs[:, :width]
    gradient_ref[...] = gradient(factor_ref[0], values_ref[...], paired_ref[...], total)
    share = jnp.max(shared_ref[...]) + unpacked(theirs, width)
    share_ref[...] = jnp.broadcast_to(share, share_ref.shape)


def text_gradient_kernel(
    whole, factor_ref, values_ref, paired_ref, pieces_ref, row_share_ref, col_share_ref,
    gradient_ref, loss_ref,
):
    total = slabs_sum(pieces_ref, values_ref.shape[0])
    gradient_ref[...] = gradient(factor_ref[0], values_ref[...], paired_ref[...], total)
    loss_ref[0] = jnp.max(row_share_ref[...] + col_share_ref[...]) * (1.0 / (LOG2_E * whole))


def exchanged(blocks, axis):
    count = lax.axis_size(axis)
    split = blocks.reshape(count, -1, blocks.shape[-1])
    return lax.all_to_all(split, axis, split_axis=0, concat_axis=0, tiled=True).reshape(blocks.shape)


def swapped(x, axis, offset=1):
    return lax.ppermute(x, axis, [(k, k ^ offset) for k in range(lax.axis_size(axis))])


def after(x, first):
    return lax.optimization_barrier((x, first))[0]


def shape(dims, dtype):
    return jax.ShapeDtypeStruct(dims, dtype)


def place(axis):
    return lax.axis_index(axis).astype(jnp.int32).reshape(1)


def on_device(image_emb, text_emb, factor):
    own_rows, width = image_emb.shape
    inner, chips = lax.axis_size(INNER), lax.axis_size(CHIPS)
    bf16, f32 = jnp.bfloat16, jnp.float32
    image_rows, text_rows = own_rows * inner, own_rows * chips
    wide = width + EXTRA
    work = 2 * image_rows * text_rows * width
    high, low = place(FAR[0]), place(FAR[1])
    tile = shape((8, 128), f32)

    text_copies = kernel_call(text_units_kernel, shape((text_rows, width), bf16), text_emb)
    text_own = exchanged(text_copies, CHIPS)
    text_other = swapped(text_own, CORE)
    half, diagonal = kernel_call(
        image_units_kernel, (shape((own_rows, width), bf16), tile), image_emb, text_emb
    )
    two = kernel_call(
        join_kernel, shape((2 * own_rows, width), bf16), low, half, swapped(half, FAR, 1)
    )
    image_copies = kernel_call(
        join_kernel, shape((image_rows, width), bf16), high, two, swapped(two, FAR, 3)
    )
    image_group = exchanged(after(image_copies, text_own), NEAR)

    tile_of = (factor, image_group, text_own, text_other)
    row_message = kernel_call(
        rows_kernel, shape((inner, 8, 128), f32), *tile_of, diagonal, flops=2 * work
    )
    row_pieces = exchanged(row_message, INNER)
    col_part = kernel_call(columns_kernel, tile, *tile_of, flops=2 * work)
    pair = kernel_call(pair_columns_kernel, tile, col_part, swapped(col_part, CORE))
    col_message = kernel_call(
        message_kernel, shape((chips, 8, 128), f32), row_pieces, pair
    )
    col_pieces = exchanged(col_message, CHIPS)

    half_tile = shape((image_rows, text_rows), bf16)
    image_part, *weights, row_share = kernel_call(
        weights_kernel,
        (shape((image_rows, wide), bf16), half_tile, half_tile, tile),
        *tile_of, row_pieces, col_pieces,
        flops=4 * work,
    )
    own_part, other_part = kernel_call(
        text_sums_kernel,
        (shape((text_rows, width), f32), shape((text_rows, wide), bf16)),
        image_group, *weights, row_share,
        flops=2 * work,
    )
    image_pieces = exchanged(image_part, NEAR)
    text_part, row_share = kernel_call(
        pair_sums_kernel, (shape((text_rows, width), bf16), tile),
        own_part, swapped(other_part, CORE), row_share,
    )
    text_pieces = exchanged(after(text_part, image_pieces), CHIPS)

    kept, sent, share = kernel_call(
        near_sums_kernel,
        (shape((2 * own_rows, width), f32), shape((2 * own_rows, wide), bf16), tile),
        high, image_pieces,
    )
    kept, sent, share = kernel_call(
        middle_sums_kernel,
        (shape((own_rows, width), f32), shape((own_rows, wide), bf16), tile),
        low, kept, swapped(sent, FAR, 3), share,
    )
    out = shape((own_rows, width), f32)
    image_grad, share = kernel_call(
        image_gradient_kernel, (out, tile),
        factor, image_emb, text_emb, kept, swapped(sent, FAR, 1), share,
    )
    whole = 2.0 * own_rows * inner * chips * lax.axis_size(CORE)
    text_grad, mean_loss = kernel_call(
        functools.partial(text_gradient_kernel, whole), (out, shape((1,), f32)),
        factor, text_emb, image_emb, text_pieces, row_share, share,
    )
    return (mean_loss, image_grad, text_grad)


def solution(mesh):
    split = Mesh(mesh.devices.reshape(2, 2, 2, 2, 4, 2, 2, 2), ALL)
    in_specs = (P(ALL, None), P(ALL, None), P())
    out_specs = (P(), P(ALL, None), P(ALL, None))
    return jax.shard_map(
        on_device, mesh=split, in_specs=in_specs, out_specs=out_specs, check_vma=False
    )
```

```python
import functools

import jax
import jax.numpy as jnp
from jax import lax
from jax.experimental import pallas as pl
from jax.experimental.pallas import tpu as pltpu
from jax.sharding import Mesh
from jax.sharding import PartitionSpec as P

ALL = ("z0", "y2", "y1", "y0", "x", "z2", "z1", "c")
INNER = ("z2", "z1", "z0", "y0")
CHIPS = ("x", "y2", "y1")
NEAR = ("z0", "y0")
FAR = ("z2", "z1")
CORE = "c"

EPSILON = 1e-06
LAST = (((1,), (1,)), ((), ()))
FIRST = (((0,), (0,)), ((), ()))
VMEM_LIMIT = 24 * 1024 * 1024
EXTRA = 128
LOG2_E = 1.4426950408889634


def f32_dot(a, b, dims):
    return lax.dot_general(a, b, dims, preferred_element_type=jnp.float32)


def unit_rows(values):
    inverse = lax.rsqrt(jnp.sum(values * values, axis=1, keepdims=True) + EPSILON)
    return values * inverse, inverse


def kernel_call(body, out_shape, *args, flops=0):
    def spec(a):
        return pl.BlockSpec(memory_space=pltpu.SMEM if a.size == 1 else pltpu.VMEM)

    outs = jax.tree.leaves(out_shape)
    moved = sum(a.size * a.dtype.itemsize for a in (*args, *outs))
    return pl.pallas_call(
        body,
        out_shape=out_shape,
        in_specs=[spec(a) for a in args],
        out_specs=jax.tree.map(spec, out_shape),
        compiler_params=pltpu.CompilerParams(vmem_limit_bytes=VMEM_LIMIT),
        cost_estimate=pl.CostEstimate(flops=flops, bytes_accessed=moved, transcendentals=0),
    )(*args)


def packed(value, rows):
    value = jnp.broadcast_to(value, (rows, EXTRA))
    high = value.astype(jnp.bfloat16).astype(jnp.float32)
    middle = (value - high).astype(jnp.bfloat16).astype(jnp.float32)
    low = value - high - middle
    lane = lax.broadcasted_iota(jnp.int32, (rows, EXTRA), 1)
    parts = jnp.where(lane == 0, high, jnp.where(lane == 1, middle, jnp.where(lane == 2, low, 0.0)))
    return parts.astype(jnp.bfloat16)


def unpacked(values, width):
    return jnp.sum(values[0:1, width:])


def text_units_kernel(values_ref, copies_ref):
    unit, _ = unit_rows(values_ref[...])
    half = jnp.concatenate([unit, unit], axis=0).astype(jnp.bfloat16)
    rows = half.shape[0]
    for k in range(copies_ref.shape[0] // rows):
        copies_ref[k * rows : (k + 1) * rows, :] = half


def image_units_kernel(values_ref, other_ref, half_ref, diagonal_ref):
    first = unit_rows(values_ref[...])[0].astype(jnp.bfloat16)
    second = unit_rows(other_ref[...])[0].astype(jnp.bfloat16)
    half_ref[...] = first
    products = first.astype(jnp.float32) * second.astype(jnp.float32)
    diagonal_ref[...] = jnp.broadcast_to(jnp.sum(products), diagonal_ref.shape)


def join_kernel(side_ref, mine_ref, theirs_ref, joined_ref):
    mine, theirs = mine_ref[...].astype(jnp.float32), theirs_ref[...].astype(jnp.float32)
    first = side_ref[0] == 0
    joined = jnp.concatenate(
        [jnp.where(first, mine, theirs), jnp.where(first, theirs, mine)], axis=0
    ).astype(jnp.bfloat16)
    rows = joined.shape[0]
    for k in range(joined_ref.shape[0] // rows):
        joined_ref[k * rows : (k + 1) * rows, :] = joined


def lines(row):
    return [row[:, k * 128 : (k + 1) * 128] for k in range(row.shape[1] // 128)]


def line(rows):
    return jnp.concatenate([rows[k : k + 1, :] for k in range(rows.shape[0])], axis=1)


def eight(rows):
    zero = jnp.zeros((1, 128), jnp.float32)
    return jnp.concatenate([*rows, *[zero] * (8 - len(rows))], axis=0)


def lse_of(logits):
    peak = jnp.max(logits, axis=0, keepdims=True)
    return peak + jnp.log2(jnp.sum(jnp.exp2(logits - peak), axis=0, keepdims=True))


def pieces_lse(pieces):
    peak = jnp.max(pieces, axis=0)
    return peak + jnp.log2(jnp.sum(jnp.exp2(pieces - peak[None]), axis=0))


def pair_lse(a, b):
    peak = jnp.maximum(a, b)
    return peak + jnp.log2(jnp.exp2(a - peak) + jnp.exp2(b - peak))


def rows_kernel(factor_ref, image_ref, own_ref, other_ref, diagonal_ref, message_ref):
    factor = factor_ref[0] * LOG2_E
    image = image_ref[...]
    own, other = (
        lse_of(factor * f32_dot(text[...], image, LAST)) for text in (own_ref, other_ref)
    )
    message = eight([*lines(pair_lse(own, other)), factor * diagonal_ref[0:1, :]])
    message_ref[...] = jnp.broadcast_to(message[None], message_ref.shape)


def columns_kernel(factor_ref, image_ref, own_ref, other_ref, message_ref):
    factor = factor_ref[0] * LOG2_E
    image = image_ref[...]
    own, other = (
        lse_of(factor * f32_dot(image, text[...], LAST)) for text in (own_ref, other_ref)
    )
    message_ref[...] = eight([*lines(own), *lines(other)])


def pair_columns_kernel(mine_ref, theirs_ref, pair_ref):
    mine, theirs = mine_ref[...], theirs_ref[...]
    own = pair_lse(mine[0:3], theirs[3:6])
    other = pair_lse(mine[3:6], theirs[0:3])
    pair_ref[...] = jnp.concatenate([own, other, jnp.zeros((2, 128), jnp.float32)], axis=0)


def message_kernel(row_ref, pair_ref, message_ref):
    pieces = row_ref[...]
    share = jnp.sum(pieces_lse(pieces)[0:3]) - 2.0 * jnp.max(jnp.sum(pieces, axis=0)[3:4])
    number = lax.broadcasted_iota(jnp.int32, (8, 128), 0)
    message = jnp.where(number == 6, share, pair_ref[...])
    message_ref[...] = jnp.broadcast_to(message[None], message_ref.shape)


def weights_kernel(
    factor_ref, image_ref, own_ref, other_ref, row_ref, pieces_ref,
    image_out, own_out, other_out, share_ref,
):
    factor = factor_ref[0]
    width = own_ref.shape[1]
    pieces = pieces_ref[...]
    cols = pieces_lse(pieces)
    own_lse, other_lse = line(cols[0:3]), line(cols[3:6])
    col_share = jnp.sum(own_lse) + jnp.sum(other_lse)
    rows = pieces_lse(row_ref[...])[0:3]
    row_share = jnp.max(jnp.sum(pieces, axis=0)[6:7])
    share_ref[...] = jnp.broadcast_to(row_share, share_ref.shape)
    row_lse = jnp.concatenate(
        [jnp.transpose(jnp.broadcast_to(rows[k : k + 1, :], (128, 128))) for k in range(3)], axis=0
    )[:, 0:1]
    image = image_ref[...]
    sums = []
    for text_ref, weights_ref, col_lse in (
        (own_ref, own_out, own_lse), (other_ref, other_out, other_lse)
    ):
        text = text_ref[...]
        logits = (factor * LOG2_E) * f32_dot(image, text, LAST)
        weights = (
            (0.5 * factor) * (jnp.exp2(logits - row_lse) + jnp.exp2(logits - col_lse))
        ).astype(jnp.bfloat16)
        weights_ref[...] = weights
        sums.append(jnp.dot(weights, text, preferred_element_type=jnp.float32))
    image_out[:, :width] = (sums[0] + sums[1]).astype(jnp.bfloat16)
    image_out[:, width:] = packed(col_share, image_out.shape[0])


def other_sums_kernel(image_ref, weights_ref, share_ref, sums_ref):
    image = image_ref[...]
    width = image.shape[1]
    sums_ref[:, :width] = f32_dot(weights_ref[...], image, FIRST).astype(jnp.bfloat16)
    sums_ref[:, width:] = packed(jnp.max(share_ref[...]), sums_ref.shape[0])


def own_sums_kernel(image_ref, weights_ref, sums_ref):
    sums_ref[...] = f32_dot(weights_ref[...], image_ref[...], FIRST)


def pair_sums_kernel(own_ref, theirs_ref, shared_ref, sums_ref, share_ref):
    width = own_ref.shape[1]
    theirs = theirs_ref[...].astype(jnp.float32)
    sums_ref[...] = (own_ref[...] + theirs[:, :width]).astype(jnp.bfloat16)
    share = jnp.max(shared_ref[...]) + unpacked(theirs, width)
    share_ref[...] = jnp.broadcast_to(share, share_ref.shape)


def slabs_sum(pieces_ref, rows):
    total = None
    for k in range(pieces_ref.shape[0] // (2 * rows)):
        both = pieces_ref[2 * rows * k : 2 * rows * (k + 1), :].astype(jnp.float32)
        both = both[:rows] + both[rows:]
        total = both if total is None else total + both
    return total


def keep_and_send(total, share, side_ref, keep_ref, send_ref, share_ref):
    rows, width = keep_ref.shape
    first = side_ref[0] == 0
    lower, upper = total[:rows, :width], total[rows:, :width]
    keep_ref[...] = jnp.where(first, lower, upper)
    send_ref[:, :width] = jnp.where(first, upper, lower).astype(jnp.bfloat16)
    send_ref[:, width:] = packed(share, rows)
    share_ref[...] = jnp.broadcast_to(share, share_ref.shape)


def near_sums_kernel(side_ref, pieces_ref, keep_ref, send_ref, share_ref):
    rows, width = keep_ref.shape
    total = slabs_sum(pieces_ref, 2 * rows)
    keep_and_send(total, unpacked(total, width), side_ref, keep_ref, send_ref, share_ref)


def middle_sums_kernel(side_ref, kept_ref, theirs_ref, shared_ref, keep_ref, send_ref, share_ref):
    width = kept_ref.shape[1]
    theirs = theirs_ref[...].astype(jnp.float32)
    share = jnp.max(shared_ref[...]) + unpacked(theirs, width)
    keep_and_send(kept_ref[...] + theirs[:, :width], share, side_ref, keep_ref, send_ref, share_ref)


def gradient(factor, values, paired, total):
    unit, inverse = unit_rows(values)
    pull = total - factor * unit_rows(paired)[0].astype(jnp.bfloat16).astype(jnp.float32)
    return (pull - unit * jnp.sum(pull * unit, axis=1, keepdims=True)) * inverse


def image_gradient_kernel(
    factor_ref, values_ref, paired_ref, kept_ref, theirs_ref, shared_ref, gradient_ref, share_ref
):
    width = kept_ref.shape[1]
    theirs = theirs_ref[...].astype(jnp.float32)
    total = kept_ref[...] + theirs[:, :width]
    gradient_ref[...] = gradient(factor_ref[0], values_ref[...], paired_ref[...], total)
    share = jnp.max(shared_ref[...]) + unpacked(theirs, width)
    share_ref[...] = jnp.broadcast_to(share, share_ref.shape)


def text_gradient_kernel(
    whole, factor_ref, values_ref, paired_ref, pieces_ref, row_share_ref, col_share_ref,
    gradient_ref, loss_ref,
):
    total = slabs_sum(pieces_ref, values_ref.shape[0])
    gradient_ref[...] = gradient(factor_ref[0], values_ref[...], paired_ref[...], total)
    loss_ref[0] = jnp.max(row_share_ref[...] + col_share_ref[...]) * (1.0 / (LOG2_E * whole))


def exchanged(blocks, axis):
    count = lax.axis_size(axis)
    split = blocks.reshape(count, -1, blocks.shape[-1])
    return lax.all_to_all(split, axis, split_axis=0, concat_axis=0, tiled=True).reshape(blocks.shape)


def swapped(x, axis, offset=1):
    return lax.ppermute(x, axis, [(k, k ^ offset) for k in range(lax.axis_size(axis))])


def after(x, first):
    return lax.optimization_barrier((x, first))[0]


def shape(dims, dtype):
    return jax.ShapeDtypeStruct(dims, dtype)


def place(axis):
    return lax.axis_index(axis).astype(jnp.int32).reshape(1)


def on_device(image_emb, text_emb, factor):
    own_rows, width = image_emb.shape
    inner, chips = lax.axis_size(INNER), lax.axis_size(CHIPS)
    bf16, f32 = jnp.bfloat16, jnp.float32
    image_rows, text_rows = own_rows * inner, own_rows * chips
    wide = width + EXTRA
    work = 2 * image_rows * text_rows * width
    high, low = place(FAR[0]), place(FAR[1])
    tile = shape((8, 128), f32)

    text_copies = kernel_call(text_units_kernel, shape((text_rows, width), bf16), text_emb)
    text_own = exchanged(text_copies, CHIPS)
    text_other = swapped(text_own, CORE)
    half, diagonal = kernel_call(
        image_units_kernel, (shape((own_rows, width), bf16), tile), image_emb, text_emb
    )
    two = kernel_call(
        join_kernel, shape((2 * own_rows, width), bf16), low, half, swapped(half, FAR, 1)
    )
    image_copies = kernel_call(
        join_kernel, shape((image_rows, width), bf16), high, two, swapped(two, FAR, 3)
    )
    image_group = exchanged(after(image_copies, text_own), NEAR)

    tile_of = (factor, image_group, text_own, text_other)
    row_message = kernel_call(
        rows_kernel, shape((inner, 8, 128), f32), *tile_of, diagonal, flops=2 * work
    )
    row_pieces = exchanged(row_message, INNER)
    col_part = kernel_call(columns_kernel, tile, *tile_of, flops=2 * work)
    pair = kernel_call(pair_columns_kernel, tile, col_part, swapped(col_part, CORE))
    col_message = kernel_call(
        message_kernel, shape((chips, 8, 128), f32), row_pieces, pair
    )
    col_pieces = exchanged(col_message, CHIPS)

    half_tile = shape((image_rows, text_rows), bf16)
    image_part, own_weights, other_weights, row_share = kernel_call(
        weights_kernel,
        (shape((image_rows, wide), bf16), half_tile, half_tile, tile),
        *tile_of, row_pieces, col_pieces,
        flops=4 * work,
    )
    other_part = kernel_call(
        other_sums_kernel, shape((text_rows, wide), bf16),
        image_group, other_weights, row_share,
        flops=work,
    )
    own_part = kernel_call(
        own_sums_kernel, shape((text_rows, width), f32), image_group, own_weights, flops=work
    )
    image_pieces = exchanged(image_part, NEAR)
    text_part, row_share = kernel_call(
        pair_sums_kernel, (shape((text_rows, width), bf16), tile),
        own_part, swapped(other_part, CORE), row_share,
    )
    text_pieces = exchanged(after(text_part, image_pieces), CHIPS)

    kept, sent, share = kernel_call(
        near_sums_kernel,
        (shape((2 * own_rows, width), f32), shape((2 * own_rows, wide), bf16), tile),
        high, image_pieces,
    )
    kept, sent, share = kernel_call(
        middle_sums_kernel,
        (shape((own_rows, width), f32), shape((own_rows, wide), bf16), tile),
        low, kept, swapped(sent, FAR, 3), share,
    )
    out = shape((own_rows, width), f32)
    image_grad, share = kernel_call(
        image_gradient_kernel, (out, tile),
        factor, image_emb, text_emb, kept, swapped(sent, FAR, 1), share,
    )
    whole = 2.0 * own_rows * inner * chips * lax.axis_size(CORE)
    text_grad, mean_loss = kernel_call(
        functools.partial(text_gradient_kernel, whole), (out, shape((1,), f32)),
        factor, text_emb, image_emb, text_pieces, row_share, share,
    )
    return (mean_loss, image_grad, text_grad)


def solution(mesh):
    split = Mesh(mesh.devices.reshape(2, 2, 2, 2, 4, 2, 2, 2), ALL)
    in_specs = (P(ALL, None), P(ALL, None), P())
    out_specs = (P(), P(ALL, None), P(ALL, None))
    return jax.shard_map(
        on_device, mesh=split, in_specs=in_specs, out_specs=out_specs, check_vma=False
    )
```

```python
import functools

import jax
import jax.numpy as jnp
from jax import lax
from jax.experimental import pallas as pl
from jax.experimental.pallas import tpu as pltpu
from jax.sharding import Mesh
from jax.sharding import PartitionSpec as P

ALL = ("z0", "y2", "y1", "y0", "x", "z2", "z1", "c")
INNER = ("z2", "z1", "z0", "y0")
CHIPS = ("x", "y2", "y1")
NEAR = ("z0", "y0")
FAR = ("z2", "z1")
CORE = "c"
BLOCK = (*CHIPS, CORE)

EPSILON = 1e-06
LAST = (((1,), (1,)), ((), ()))
FIRST = (((0,), (0,)), ((), ()))
VMEM_LIMIT = 24 * 1024 * 1024
EXTRA = 128
LOG2_E = 1.4426950408889634


def f32_dot(a, b, dims):
    return lax.dot_general(a, b, dims, preferred_element_type=jnp.float32)


def unit_rows(values):
    inverse = lax.rsqrt(jnp.sum(values * values, axis=1, keepdims=True) + EPSILON)
    return values * inverse, inverse


def kernel_call(body, out_shape, *args, flops=0):
    def spec(a):
        return pl.BlockSpec(memory_space=pltpu.SMEM if a.size == 1 else pltpu.VMEM)

    outs = jax.tree.leaves(out_shape)
    moved = sum(a.size * a.dtype.itemsize for a in (*args, *outs))
    return pl.pallas_call(
        body,
        out_shape=out_shape,
        in_specs=[spec(a) for a in args],
        out_specs=jax.tree.map(spec, out_shape),
        compiler_params=pltpu.CompilerParams(vmem_limit_bytes=VMEM_LIMIT),
        cost_estimate=pl.CostEstimate(flops=flops, bytes_accessed=moved, transcendentals=0),
    )(*args)


def packed(value, rows):
    value = jnp.broadcast_to(value, (rows, EXTRA))
    high = value.astype(jnp.bfloat16).astype(jnp.float32)
    middle = (value - high).astype(jnp.bfloat16).astype(jnp.float32)
    low = value - high - middle
    lane = lax.broadcasted_iota(jnp.int32, (rows, EXTRA), 1)
    parts = jnp.where(lane == 0, high, jnp.where(lane == 1, middle, jnp.where(lane == 2, low, 0.0)))
    return parts.astype(jnp.bfloat16)


def unpacked(values, width):
    return jnp.sum(values[0:1, width:])


def text_units_kernel(values_ref, copies_ref):
    unit, _ = unit_rows(values_ref[...])
    half = jnp.concatenate([unit, unit], axis=0).astype(jnp.bfloat16)
    rows = half.shape[0]
    for k in range(copies_ref.shape[0] // rows):
        copies_ref[k * rows : (k + 1) * rows, :] = half


def image_units_kernel(values_ref, other_ref, half_ref, diagonal_ref):
    first = unit_rows(values_ref[...])[0].astype(jnp.bfloat16)
    second = unit_rows(other_ref[...])[0].astype(jnp.bfloat16)
    half_ref[...] = first
    products = first.astype(jnp.float32) * second.astype(jnp.float32)
    diagonal_ref[...] = jnp.broadcast_to(jnp.sum(products), diagonal_ref.shape)


def join_kernel(side_ref, mine_ref, theirs_ref, joined_ref):
    mine, theirs = mine_ref[...].astype(jnp.float32), theirs_ref[...].astype(jnp.float32)
    first = side_ref[0] == 0
    joined = jnp.concatenate(
        [jnp.where(first, mine, theirs), jnp.where(first, theirs, mine)], axis=0
    ).astype(jnp.bfloat16)
    rows = joined.shape[0]
    for k in range(joined_ref.shape[0] // rows):
        joined_ref[k * rows : (k + 1) * rows, :] = joined


def lines(row):
    return [row[:, k * 128 : (k + 1) * 128] for k in range(row.shape[1] // 128)]


def line(rows):
    return jnp.concatenate([rows[k : k + 1, :] for k in range(rows.shape[0])], axis=1)


def eight(rows):
    zero = jnp.zeros((1, 128), jnp.float32)
    return jnp.concatenate([*rows, *[zero] * (8 - len(rows))], axis=0)


def lse_of(logits):
    peak = jnp.max(logits, axis=0, keepdims=True)
    return peak + jnp.log2(jnp.sum(jnp.exp2(logits - peak), axis=0, keepdims=True))


def pieces_lse(pieces):
    peak = jnp.max(pieces, axis=0)
    return peak + jnp.log2(jnp.sum(jnp.exp2(pieces - peak[None]), axis=0))


def pair_lse(a, b):
    peak = jnp.maximum(a, b)
    return peak + jnp.log2(jnp.exp2(a - peak) + jnp.exp2(b - peak))


def rows_kernel(factor_ref, image_ref, own_ref, other_ref, diagonal_ref, message_ref):
    factor = factor_ref[0] * LOG2_E
    image = image_ref[...]
    own, other = (
        lse_of(factor * f32_dot(text[...], image, LAST)) for text in (own_ref, other_ref)
    )
    message = eight([*lines(pair_lse(own, other)), factor * diagonal_ref[0:1, :]])
    message_ref[...] = jnp.broadcast_to(message[None], message_ref.shape)


def columns_kernel(factor_ref, image_ref, own_ref, other_ref, core_ref, message_ref):
    factor = factor_ref[0] * LOG2_E
    image = image_ref[...]
    own, other = (
        lse_of(factor * f32_dot(image, text[...], LAST)) for text in (own_ref, other_ref)
    )
    first = core_ref[0] == 0
    message_ref[...] = eight(
        [*lines(jnp.where(first, own, other)), *lines(jnp.where(first, other, own))]
    )


def message_kernel(row_ref, columns_ref, message_ref):
    pieces = row_ref[...]
    share = jnp.sum(pieces_lse(pieces)[0:3]) - 2.0 * jnp.max(jnp.sum(pieces, axis=0)[3:4])
    number = lax.broadcasted_iota(jnp.int32, (8, 128), 0)
    message = jnp.where(number == 6, share, columns_ref[...])
    message_ref[...] = jnp.broadcast_to(message[None], message_ref.shape)


def weights_kernel(
    factor_ref, image_ref, own_ref, other_ref, core_ref, row_ref, pieces_ref,
    image_out, own_out, other_out, share_ref,
):
    factor = factor_ref[0]
    width = own_ref.shape[1]
    pieces = pieces_ref[...]
    cols = pieces_lse(pieces)
    low_lse, high_lse = line(cols[0:3]), line(cols[3:6])
    first = core_ref[0] == 0
    own_lse, other_lse = jnp.where(first, low_lse, high_lse), jnp.where(first, high_lse, low_lse)
    col_share = jnp.sum(low_lse) + jnp.sum(high_lse)
    rows = pieces_lse(row_ref[...])[0:3]
    row_share = jnp.max(jnp.sum(pieces, axis=0)[6:7])
    share_ref[...] = jnp.broadcast_to(row_share, share_ref.shape)
    row_lse = jnp.concatenate(
        [jnp.transpose(jnp.broadcast_to(rows[k : k + 1, :], (128, 128))) for k in range(3)], axis=0
    )[:, 0:1]
    image = image_ref[...]
    sums = []
    for text_ref, weights_ref, col_lse in (
        (own_ref, own_out, own_lse), (other_ref, other_out, other_lse)
    ):
        text = text_ref[...]
        logits = (factor * LOG2_E) * f32_dot(image, text, LAST)
        weights = (
            (0.5 * factor) * (jnp.exp2(logits - row_lse) + jnp.exp2(logits - col_lse))
        ).astype(jnp.bfloat16)
        weights_ref[...] = weights
        sums.append(jnp.dot(weights, text, preferred_element_type=jnp.float32))
    image_out[:, :width] = (sums[0] + sums[1]).astype(jnp.bfloat16)
    image_out[:, width:] = packed(col_share, image_out.shape[0])


def other_sums_kernel(image_ref, weights_ref, sums_ref):
    sums_ref[...] = f32_dot(weights_ref[...], image_ref[...], FIRST).astype(jnp.bfloat16)


def own_sums_kernel(image_ref, weights_ref, sums_ref):
    sums_ref[...] = f32_dot(weights_ref[...], image_ref[...], FIRST)


def pair_sums_kernel(own_ref, theirs_ref, sums_ref):
    sums_ref[...] = (own_ref[...] + theirs_ref[...].astype(jnp.float32)).astype(jnp.bfloat16)


def slabs_sum(pieces_ref, rows):
    total = None
    for k in range(pieces_ref.shape[0] // (2 * rows)):
        both = pieces_ref[2 * rows * k : 2 * rows * (k + 1), :].astype(jnp.float32)
        both = both[:rows] + both[rows:]
        total = both if total is None else total + both
    return total


def keep_and_send(total, share, side_ref, keep_ref, send_ref, share_ref):
    rows, width = keep_ref.shape
    first = side_ref[0] == 0
    lower, upper = total[:rows, :width], total[rows:, :width]
    keep_ref[...] = jnp.where(first, lower, upper)
    send_ref[:, :width] = jnp.where(first, upper, lower).astype(jnp.bfloat16)
    send_ref[:, width:] = packed(share, rows)
    share_ref[...] = jnp.broadcast_to(share, share_ref.shape)


def near_sums_kernel(side_ref, pieces_ref, keep_ref, send_ref, share_ref):
    rows, width = keep_ref.shape
    total = slabs_sum(pieces_ref, 2 * rows)
    keep_and_send(total, unpacked(total, width), side_ref, keep_ref, send_ref, share_ref)


def middle_sums_kernel(side_ref, kept_ref, theirs_ref, shared_ref, keep_ref, send_ref, share_ref):
    width = kept_ref.shape[1]
    theirs = theirs_ref[...].astype(jnp.float32)
    share = jnp.max(shared_ref[...]) + unpacked(theirs, width)
    keep_and_send(kept_ref[...] + theirs[:, :width], share, side_ref, keep_ref, send_ref, share_ref)


def gradient(factor, values, paired, total):
    unit, inverse = unit_rows(values)
    pull = total - factor * unit_rows(paired)[0].astype(jnp.bfloat16).astype(jnp.float32)
    return (pull - unit * jnp.sum(pull * unit, axis=1, keepdims=True)) * inverse


def image_gradient_kernel(
    factor_ref, values_ref, paired_ref, kept_ref, theirs_ref, shared_ref, gradient_ref, share_ref
):
    width = kept_ref.shape[1]
    theirs = theirs_ref[...].astype(jnp.float32)
    total = kept_ref[...] + theirs[:, :width]
    gradient_ref[...] = gradient(factor_ref[0], values_ref[...], paired_ref[...], total)
    share = jnp.max(shared_ref[...]) + unpacked(theirs, width)
    share_ref[...] = jnp.broadcast_to(share, share_ref.shape)


def text_gradient_kernel(
    whole, factor_ref, values_ref, paired_ref, pieces_ref, row_share_ref, col_share_ref,
    gradient_ref, loss_ref,
):
    total = slabs_sum(pieces_ref, values_ref.shape[0])
    gradient_ref[...] = gradient(factor_ref[0], values_ref[...], paired_ref[...], total)
    loss_ref[0] = jnp.max(row_share_ref[...] + col_share_ref[...]) * (1.0 / (LOG2_E * whole))


def exchanged(blocks, axis):
    count = lax.axis_size(axis)
    split = blocks.reshape(count, -1, blocks.shape[-1])
    return lax.all_to_all(split, axis, split_axis=0, concat_axis=0, tiled=True).reshape(blocks.shape)


def swapped(x, axis, offset=1):
    return lax.ppermute(x, axis, [(k, k ^ offset) for k in range(lax.axis_size(axis))])


def after(x, first):
    return lax.optimization_barrier((x, first))[0]


def shape(dims, dtype):
    return jax.ShapeDtypeStruct(dims, dtype)


def place(axis):
    return lax.axis_index(axis).astype(jnp.int32).reshape(1)


def on_device(image_emb, text_emb, factor):
    own_rows, width = image_emb.shape
    inner, chips = lax.axis_size(INNER), lax.axis_size(CHIPS)
    bf16, f32 = jnp.bfloat16, jnp.float32
    image_rows, text_rows = own_rows * inner, own_rows * chips
    wide = width + EXTRA
    work = 2 * image_rows * text_rows * width
    high, low, core = place(FAR[0]), place(FAR[1]), place(CORE)
    tile = shape((8, 128), f32)

    text_copies = kernel_call(text_units_kernel, shape((text_rows, width), bf16), text_emb)
    text_own = exchanged(text_copies, CHIPS)
    text_other = swapped(text_own, CORE)
    half, diagonal = kernel_call(
        image_units_kernel, (shape((own_rows, width), bf16), tile), image_emb, text_emb
    )
    two = kernel_call(
        join_kernel, shape((2 * own_rows, width), bf16), low, half, swapped(half, FAR, 1)
    )
    image_copies = kernel_call(
        join_kernel, shape((image_rows, width), bf16), high, two, swapped(two, FAR, 3)
    )
    image_group = exchanged(after(image_copies, text_own), NEAR)

    tile_of = (factor, image_group, text_own, text_other)
    row_message = kernel_call(
        rows_kernel, shape((inner, 8, 128), f32), *tile_of, diagonal, flops=2 * work
    )
    row_pieces = exchanged(row_message, INNER)
    col_part = kernel_call(columns_kernel, tile, *tile_of, core, flops=2 * work)
    col_message = kernel_call(
        message_kernel, shape((lax.axis_size(BLOCK), 8, 128), f32), row_pieces, col_part
    )
    col_pieces = exchanged(col_message, BLOCK)

    half_tile = shape((image_rows, text_rows), bf16)
    image_part, own_weights, other_weights, row_share = kernel_call(
        weights_kernel,
        (shape((image_rows, wide), bf16), half_tile, half_tile, tile),
        *tile_of, core, row_pieces, col_pieces,
        flops=4 * work,
    )
    other_part = kernel_call(
        other_sums_kernel, shape((text_rows, width), bf16), image_group, other_weights,
        flops=work,
    )
    own_part = kernel_call(
        own_sums_kernel, shape((text_rows, width), f32), image_group, own_weights, flops=work
    )
    image_pieces = exchanged(image_part, NEAR)
    text_part = kernel_call(
        pair_sums_kernel, shape((text_rows, width), bf16), own_part, swapped(other_part, CORE)
    )
    text_pieces = exchanged(after(text_part, image_pieces), CHIPS)

    kept, sent, share = kernel_call(
        near_sums_kernel,
        (shape((2 * own_rows, width), f32), shape((2 * own_rows, wide), bf16), tile),
        high, image_pieces,
    )
    kept, sent, share = kernel_call(
        middle_sums_kernel,
        (shape((own_rows, width), f32), shape((own_rows, wide), bf16), tile),
        low, kept, swapped(sent, FAR, 3), share,
    )
    out = shape((own_rows, width), f32)
    image_grad, share = kernel_call(
        image_gradient_kernel, (out, tile),
        factor, image_emb, text_emb, kept, swapped(sent, FAR, 1), share,
    )
    whole = 2.0 * own_rows * inner * chips * lax.axis_size(CORE)
    text_grad, mean_loss = kernel_call(
        functools.partial(text_gradient_kernel, whole), (out, shape((1,), f32)),
        factor, text_emb, image_emb, text_pieces, row_share, share,
    )
    return (mean_loss, image_grad, text_grad)


def solution(mesh):
    split = Mesh(mesh.devices.reshape(2, 2, 2, 2, 4, 2, 2, 2), ALL)
    in_specs = (P(ALL, None), P(ALL, None), P())
    out_specs = (P(), P(ALL, None), P(ALL, None))
    return jax.shard_map(
        on_device, mesh=split, in_specs=in_specs, out_specs=out_specs, check_vma=False
    )
```

```python
import functools

import jax
import jax.numpy as jnp
from jax import lax
from jax.experimental import pallas as pl
from jax.experimental.pallas import tpu as pltpu
from jax.sharding import Mesh
from jax.sharding import PartitionSpec as P

ALL = ("z0", "y2", "y1", "y0", "x", "z2", "z1", "c")
INNER = ("z2", "z1", "z0", "y0")
CHIPS = ("y2", "y1", "x")
NEAR = ("z0", "y0")
FAR = ("z2", "z1")
CORE = "c"

EPSILON = 1e-06
LAST = (((1,), (1,)), ((), ()))
FIRST = (((0,), (0,)), ((), ()))
VMEM_LIMIT = 24 * 1024 * 1024
EXTRA = 128
LOG2_E = 1.4426950408889634


def f32_dot(a, b, dims):
    return lax.dot_general(a, b, dims, preferred_element_type=jnp.float32)


def unit_rows(values):
    inverse = lax.rsqrt(jnp.sum(values * values, axis=1, keepdims=True) + EPSILON)
    return values * inverse, inverse


def kernel_call(body, out_shape, *args, flops=0):
    def spec(a):
        return pl.BlockSpec(memory_space=pltpu.SMEM if a.size == 1 else pltpu.VMEM)

    outs = jax.tree.leaves(out_shape)
    moved = sum(a.size * a.dtype.itemsize for a in (*args, *outs))
    return pl.pallas_call(
        body,
        out_shape=out_shape,
        in_specs=[spec(a) for a in args],
        out_specs=jax.tree.map(spec, out_shape),
        compiler_params=pltpu.CompilerParams(vmem_limit_bytes=VMEM_LIMIT),
        cost_estimate=pl.CostEstimate(flops=flops, bytes_accessed=moved, transcendentals=0),
    )(*args)


def packed(value, rows):
    value = jnp.broadcast_to(value, (rows, EXTRA))
    high = value.astype(jnp.bfloat16).astype(jnp.float32)
    middle = (value - high).astype(jnp.bfloat16).astype(jnp.float32)
    low = value - high - middle
    lane = lax.broadcasted_iota(jnp.int32, (rows, EXTRA), 1)
    parts = jnp.where(lane == 0, high, jnp.where(lane == 1, middle, jnp.where(lane == 2, low, 0.0)))
    return parts.astype(jnp.bfloat16)


def unpacked(values, width):
    return jnp.sum(values[0:1, width:])


def text_units_kernel(values_ref, copies_ref):
    unit, _ = unit_rows(values_ref[...])
    half = jnp.concatenate([unit, unit], axis=0).astype(jnp.bfloat16)
    rows = half.shape[0]
    for k in range(copies_ref.shape[0] // rows):
        copies_ref[k * rows : (k + 1) * rows, :] = half


def image_units_kernel(values_ref, other_ref, half_ref, diagonal_ref):
    first = unit_rows(values_ref[...])[0].astype(jnp.bfloat16)
    second = unit_rows(other_ref[...])[0].astype(jnp.bfloat16)
    half_ref[...] = first
    products = first.astype(jnp.float32) * second.astype(jnp.float32)
    diagonal_ref[...] = jnp.broadcast_to(jnp.sum(products), diagonal_ref.shape)


def join_kernel(side_ref, mine_ref, theirs_ref, joined_ref):
    mine, theirs = mine_ref[...].astype(jnp.float32), theirs_ref[...].astype(jnp.float32)
    first = side_ref[0] == 0
    joined = jnp.concatenate(
        [jnp.where(first, mine, theirs), jnp.where(first, theirs, mine)], axis=0
    ).astype(jnp.bfloat16)
    rows = joined.shape[0]
    for k in range(joined_ref.shape[0] // rows):
        joined_ref[k * rows : (k + 1) * rows, :] = joined


def lines(row):
    return [row[:, k * 128 : (k + 1) * 128] for k in range(row.shape[1] // 128)]


def line(rows):
    return jnp.concatenate([rows[k : k + 1, :] for k in range(rows.shape[0])], axis=1)


def eight(rows):
    zero = jnp.zeros((1, 128), jnp.float32)
    return jnp.concatenate([*rows, *[zero] * (8 - len(rows))], axis=0)


def lse_of(logits):
    peak = jnp.max(logits, axis=0, keepdims=True)
    return peak + jnp.log2(jnp.sum(jnp.exp2(logits - peak), axis=0, keepdims=True))


def pieces_lse(pieces):
    peak = jnp.max(pieces, axis=0)
    return peak + jnp.log2(jnp.sum(jnp.exp2(pieces - peak[None]), axis=0))


def pair_lse(a, b):
    peak = jnp.maximum(a, b)
    return peak + jnp.log2(jnp.exp2(a - peak) + jnp.exp2(b - peak))


def rows_kernel(factor_ref, image_ref, own_ref, other_ref, diagonal_ref, message_ref):
    factor = factor_ref[0] * LOG2_E
    image = image_ref[...]
    own, other = (
        lse_of(factor * f32_dot(text[...], image, LAST)) for text in (own_ref, other_ref)
    )
    message = eight([*lines(pair_lse(own, other)), factor * diagonal_ref[0:1, :]])
    message_ref[...] = jnp.broadcast_to(message[None], message_ref.shape)


def columns_kernel(factor_ref, image_ref, own_ref, other_ref, message_ref):
    factor = factor_ref[0] * LOG2_E
    image = image_ref[...]
    own, other = (
        lse_of(factor * f32_dot(image, text[...], LAST)) for text in (own_ref, other_ref)
    )
    message_ref[...] = eight([*lines(own), *lines(other)])


def pair_columns_kernel(mine_ref, theirs_ref, pair_ref):
    mine, theirs = mine_ref[...], theirs_ref[...]
    own = pair_lse(mine[0:3], theirs[3:6])
    other = pair_lse(mine[3:6], theirs[0:3])
    pair_ref[...] = jnp.concatenate([own, other, jnp.zeros((2, 128), jnp.float32)], axis=0)


def message_kernel(row_ref, pair_ref, message_ref):
    pieces = row_ref[...]
    share = jnp.sum(pieces_lse(pieces)[0:3]) - 2.0 * jnp.max(jnp.sum(pieces, axis=0)[3:4])
    number = lax.broadcasted_iota(jnp.int32, (8, 128), 0)
    message = jnp.where(number == 6, share, pair_ref[...])
    message_ref[...] = jnp.broadcast_to(message[None], message_ref.shape)


def weights_kernel(
    factor_ref, image_ref, own_ref, other_ref, row_ref, pieces_ref,
    image_out, own_out, other_out, share_ref,
):
    factor = factor_ref[0]
    width = own_ref.shape[1]
    pieces = pieces_ref[...]
    cols = pieces_lse(pieces)
    own_lse, other_lse = line(cols[0:3]), line(cols[3:6])
    col_share = jnp.sum(own_lse) + jnp.sum(other_lse)
    rows = pieces_lse(row_ref[...])[0:3]
    row_share = jnp.max(jnp.sum(pieces, axis=0)[6:7])
    share_ref[...] = jnp.broadcast_to(row_share, share_ref.shape)
    row_lse = jnp.concatenate(
        [jnp.transpose(jnp.broadcast_to(rows[k : k + 1, :], (128, 128))) for k in range(3)], axis=0
    )[:, 0:1]
    image = image_ref[...]
    sums = []
    for text_ref, weights_ref, col_lse in (
        (own_ref, own_out, own_lse), (other_ref, other_out, other_lse)
    ):
        text = text_ref[...]
        logits = (factor * LOG2_E) * f32_dot(image, text, LAST)
        weights = (
            (0.5 * factor) * (jnp.exp2(logits - row_lse) + jnp.exp2(logits - col_lse))
        ).astype(jnp.bfloat16)
        weights_ref[...] = weights
        sums.append(jnp.dot(weights, text, preferred_element_type=jnp.float32))
    image_out[:, :width] = (sums[0] + sums[1]).astype(jnp.bfloat16)
    image_out[:, width:] = packed(col_share, image_out.shape[0])


def other_sums_kernel(image_ref, weights_ref, share_ref, sums_ref):
    image = image_ref[...]
    width = image.shape[1]
    sums_ref[:, :width] = f32_dot(weights_ref[...], image, FIRST).astype(jnp.bfloat16)
    sums_ref[:, width:] = packed(jnp.max(share_ref[...]), sums_ref.shape[0])


def own_sums_kernel(image_ref, weights_ref, sums_ref):
    sums_ref[...] = f32_dot(weights_ref[...], image_ref[...], FIRST)


def pair_sums_kernel(own_ref, theirs_ref, shared_ref, sums_ref, share_ref):
    width = own_ref.shape[1]
    theirs = theirs_ref[...].astype(jnp.float32)
    sums_ref[...] = (own_ref[...] + theirs[:, :width]).astype(jnp.bfloat16)
    share = jnp.max(shared_ref[...]) + unpacked(theirs, width)
    share_ref[...] = jnp.broadcast_to(share, share_ref.shape)


def slabs_sum(pieces_ref, rows):
    total = None
    for k in range(pieces_ref.shape[0] // (2 * rows)):
        both = pieces_ref[2 * rows * k : 2 * rows * (k + 1), :].astype(jnp.float32)
        both = both[:rows] + both[rows:]
        total = both if total is None else total + both
    return total


def keep_and_send(total, share, side_ref, keep_ref, send_ref, share_ref):
    rows, width = keep_ref.shape
    first = side_ref[0] == 0
    lower, upper = total[:rows, :width], total[rows:, :width]
    keep_ref[...] = jnp.where(first, lower, upper)
    send_ref[:, :width] = jnp.where(first, upper, lower).astype(jnp.bfloat16)
    send_ref[:, width:] = packed(share, rows)
    share_ref[...] = jnp.broadcast_to(share, share_ref.shape)


def near_sums_kernel(side_ref, pieces_ref, keep_ref, send_ref, share_ref):
    rows, width = keep_ref.shape
    total = slabs_sum(pieces_ref, 2 * rows)
    keep_and_send(total, unpacked(total, width), side_ref, keep_ref, send_ref, share_ref)


def middle_sums_kernel(side_ref, kept_ref, theirs_ref, shared_ref, keep_ref, send_ref, share_ref):
    width = kept_ref.shape[1]
    theirs = theirs_ref[...].astype(jnp.float32)
    share = jnp.max(shared_ref[...]) + unpacked(theirs, width)
    keep_and_send(kept_ref[...] + theirs[:, :width], share, side_ref, keep_ref, send_ref, share_ref)


def gradient(factor, values, paired, total):
    unit, inverse = unit_rows(values)
    pull = total - factor * unit_rows(paired)[0].astype(jnp.bfloat16).astype(jnp.float32)
    return (pull - unit * jnp.sum(pull * unit, axis=1, keepdims=True)) * inverse


def image_gradient_kernel(
    factor_ref, values_ref, paired_ref, kept_ref, theirs_ref, shared_ref, gradient_ref, share_ref
):
    width = kept_ref.shape[1]
    theirs = theirs_ref[...].astype(jnp.float32)
    total = kept_ref[...] + theirs[:, :width]
    gradient_ref[...] = gradient(factor_ref[0], values_ref[...], paired_ref[...], total)
    share = jnp.max(shared_ref[...]) + unpacked(theirs, width)
    share_ref[...] = jnp.broadcast_to(share, share_ref.shape)


def text_gradient_kernel(
    whole, factor_ref, values_ref, paired_ref, pieces_ref, row_share_ref, col_share_ref,
    gradient_ref, loss_ref,
):
    total = slabs_sum(pieces_ref, values_ref.shape[0])
    gradient_ref[...] = gradient(factor_ref[0], values_ref[...], paired_ref[...], total)
    loss_ref[0] = jnp.max(row_share_ref[...] + col_share_ref[...]) * (1.0 / (LOG2_E * whole))


def exchanged(blocks, axis):
    count = lax.axis_size(axis)
    split = blocks.reshape(count, -1, blocks.shape[-1])
    return lax.all_to_all(split, axis, split_axis=0, concat_axis=0, tiled=True).reshape(blocks.shape)


def swapped(x, axis, offset=1):
    return lax.ppermute(x, axis, [(k, k ^ offset) for k in range(lax.axis_size(axis))])


def after(x, first):
    return lax.optimization_barrier((x, first))[0]


def shape(dims, dtype):
    return jax.ShapeDtypeStruct(dims, dtype)


def place(axis):
    return lax.axis_index(axis).astype(jnp.int32).reshape(1)


def on_device(image_emb, text_emb, factor):
    own_rows, width = image_emb.shape
    inner, chips = lax.axis_size(INNER), lax.axis_size(CHIPS)
    bf16, f32 = jnp.bfloat16, jnp.float32
    image_rows, text_rows = own_rows * inner, own_rows * chips
    wide = width + EXTRA
    work = 2 * image_rows * text_rows * width
    high, low = place(FAR[0]), place(FAR[1])
    tile = shape((8, 128), f32)

    text_copies = kernel_call(text_units_kernel, shape((text_rows, width), bf16), text_emb)
    text_own = exchanged(text_copies, CHIPS)
    text_other = swapped(text_own, CORE)
    half, diagonal = kernel_call(
        image_units_kernel, (shape((own_rows, width), bf16), tile), image_emb, text_emb
    )
    two = kernel_call(
        join_kernel, shape((2 * own_rows, width), bf16), low, half, swapped(half, FAR, 1)
    )
    image_copies = kernel_call(
        join_kernel, shape((image_rows, width), bf16), high, two, swapped(two, FAR, 3)
    )
    image_group = exchanged(after(image_copies, text_own), NEAR)

    tile_of = (factor, image_group, text_own, text_other)
    row_message = kernel_call(
        rows_kernel, shape((inner, 8, 128), f32), *tile_of, diagonal, flops=2 * work
    )
    row_pieces = exchanged(row_message, INNER)
    col_part = kernel_call(columns_kernel, tile, *tile_of, flops=2 * work)
    pair = kernel_call(pair_columns_kernel, tile, col_part, swapped(col_part, CORE))
    col_message = kernel_call(
        message_kernel, shape((chips, 8, 128), f32), row_pieces, pair
    )
    col_pieces = exchanged(col_message, CHIPS)

    half_tile = shape((image_rows, text_rows), bf16)
    image_part, own_weights, other_weights, row_share = kernel_call(
        weights_kernel,
        (shape((image_rows, wide), bf16), half_tile, half_tile, tile),
        *tile_of, row_pieces, col_pieces,
        flops=4 * work,
    )
    other_part = kernel_call(
        other_sums_kernel, shape((text_rows, wide), bf16),
        image_group, other_weights, row_share,
        flops=work,
    )
    own_part = kernel_call(
        own_sums_kernel, shape((text_rows, width), f32), image_group, own_weights, flops=work
    )
    image_pieces = exchanged(image_part, NEAR)
    text_part, row_share = kernel_call(
        pair_sums_kernel, (shape((text_rows, width), bf16), tile),
        own_part, swapped(other_part, CORE), row_share,
    )
    text_pieces = exchanged(after(text_part, image_pieces), CHIPS)

    kept, sent, share = kernel_call(
        near_sums_kernel,
        (shape((2 * own_rows, width), f32), shape((2 * own_rows, wide), bf16), tile),
        high, image_pieces,
    )
    kept, sent, share = kernel_call(
        middle_sums_kernel,
        (shape((own_rows, width), f32), shape((own_rows, wide), bf16), tile),
        low, kept, swapped(sent, FAR, 3), share,
    )
    out = shape((own_rows, width), f32)
    image_grad, share = kernel_call(
        image_gradient_kernel, (out, tile),
        factor, image_emb, text_emb, kept, swapped(sent, FAR, 1), share,
    )
    whole = 2.0 * own_rows * inner * chips * lax.axis_size(CORE)
    text_grad, mean_loss = kernel_call(
        functools.partial(text_gradient_kernel, whole), (out, shape((1,), f32)),
        factor, text_emb, image_emb, text_pieces, row_share, share,
    )
    return (mean_loss, image_grad, text_grad)


def solution(mesh):
    split = Mesh(mesh.devices.reshape(2, 2, 2, 2, 4, 2, 2, 2), ALL)
    in_specs = (P(ALL, None), P(ALL, None), P())
    out_specs = (P(), P(ALL, None), P(ALL, None))
    return jax.shard_map(
        on_device, mesh=split, in_specs=in_specs, out_specs=out_specs, check_vma=False
    )
```
